32 devices in a mesh: groups: 2 (over y), brick: 4 (over z), chan: 2 (over x), sub: 2 (over core).
Axes of the slice: x: 2, y: 2, z: 4, core: 2. Of those that a mesh axis runs over, the one named last changes fastest.
Arguments:
- features: bfloat16 [16384, 256], P(('groups', 'brick', 'chan', 'sub')), parts along dimension 0, may hold values from -6 to 6
- scan_order: int32 [32, 512], P(('groups', 'brick', 'chan', 'sub')), parts along dimension 0, may hold values from 0 to 511, each once within a row
- kernel_map: int32 [256, 27], P(('groups', 'brick', 'sub')), parts along dimension 0, may hold values from 0 to 20, as said below
- halo_send: int32 [32, 2], P(('groups', 'brick', 'sub')), parts along dimension 0, may hold values from 0 to 15, as said below
- down_route: int32 [256, 1], P(('groups', 'brick', 'sub')), parts along dimension 0, may hold values from 0 to 7; in each aligned block of 16 rows (0 to 15, 16 to 31, ...) at most 4 rows name the same one
- conv1_weight: bfloat16 [27, 256, 256], P(None, 'chan'), may hold values from -0.078125 to 0.078125
- conv2_weight: bfloat16 [27, 256, 256], P(None, 'chan'), may hold values from -0.078125 to 0.078125
- down_weight: bfloat16 [8, 256, 256], P(None, 'chan'), may hold values from -0.125 to 0.125
- gain_first: float32 [256], P('chan'), may hold values from 0.1 to 1.9
- bias_first: float32 [256], P('chan'), may hold values from -3 to 3
- gain_second: float32 [256], P('chan'), may hold values from 0.1 to 1.9
- bias_second: float32 [256], P('chan'), may hold values from -3 to 3
- gain_down: float32 [256], P('chan'), may hold values from 0.1 to 1.9
- bias_down: float32 [256], P('chan'), may hold values from -3 to 3
Outputs:
- coarse_out: bfloat16 [16, 256, 256], P(('groups', 'brick', 'sub'), 'chan'), parts along dimension 0
The draws below stay inside these ranges and needn't reach their ends.
There are 2 independent parts, one for each index of `groups`. The reference program is written for one: setup_inputs(seed, part) draws one part's arguments, and reference() takes and returns one part's arrays. A program takes and returns all parts, laid end to end along the dimension named above; an argument that names none is the same for every part. Nothing has to cross between parts.
Inputs may be any that keep to these rules, and one draw needn't show every extreme that they name: `scan_order`: each row is an order of the 512 local rows of one device, each once. `kernel_map`: entries index an owner's extended list: own blocks below 16, then 2 blocks from the previous owner, 2 from the next, and 20 for an absent neighbour block. Offset 13 of block n always names n itself. `halo_send`: row 2 o lists the blocks owner o sends to owner o + 1, row 2 o + 1 those it sends to owner o - 1; each row names 2 distinct blocks. `down_route`: within the 16 rows of one owner no destination is named by more than 4 rows.
All inputs are finite; a program needn't handle non-finite values.
Results may differ from the reference program's by a relative error of at most 0.014.
Values may be sent and summed in bfloat16 or wider, within the bound.
No kernel may reach another device: no remote copies, remote signals or barrier semaphores. Data moves between devices by JAX's collectives and lax.ppermute only.
A program may use at most 64 MiB of HBM per device.

```python
import math
import jax
import jax.numpy as jnp
import numpy as np
from jax import lax

C = 256
K = 27
BLK = 64
SCAN_DEV = 512
OWNERS = 8
SCAN_DEVS = 16
SCAN_ROWS = 8192
NB_OWN = 16
HCAP = 2
NB_EXT = 20
DCAP = 4
N_BRICK = 4
N_CHAN = 2
N_SUB = 2


def draw_kernel_map(key, part):
    key_kind, key_own, key_rim = jax.random.split(key, 3)
    shape = (OWNERS, NB_OWN, K)
    choose = jax.random.randint(key_kind, shape, 0, 10)
    own_block = jax.random.randint(key_own, shape, 0, NB_OWN)
    rim_block = jax.random.randint(key_rim, shape, NB_OWN, NB_EXT)
    table = jnp.where(choose < 4, own_block, jnp.where(choose < 6, rim_block, NB_EXT))
    block_index = jnp.arange(NB_OWN, dtype=jnp.int32)[None, :, None]
    offset_index = jnp.arange(K, dtype=jnp.int32)[None, None, :]
    table = jnp.where(offset_index == 13, block_index, table)
    table = jnp.where((offset_index == 0) & (block_index < 2 * HCAP), NB_OWN + block_index, table)
    return table.reshape(OWNERS * NB_OWN, K).astype(jnp.int32)


def pick_blocks(subkey):
    return jax.random.permutation(subkey, NB_OWN)


def draw_halo_send(key, part):
    subkeys = jax.random.split(key, OWNERS * 2)
    orders = jax.vmap(pick_blocks)(subkeys)
    return orders[:, :HCAP].astype(jnp.int32)


def levels(stream_key, extent, cuts, least, largest):
    factor_of = 1.0
    for dim, blocks in cuts:
        steps = jax.random.uniform(jax.random.fold_in(jax.random.fold_in(stream_key, 6), dim), (blocks,), jnp.float32, least / len(cuts), largest / len(cuts))
        factor_of = factor_of * jnp.repeat(jnp.exp(steps), extent[dim] // blocks).reshape((-1,) + (1,) * (len(extent) - 1 - dim))
    return factor_of


def shared_out(rng, own, number, rows, amount, top, limit, skew):
    ranking = jax.random.permutation(rng, amount)
    crowded, usual = portions_of(amount, rows * top, limit, skew, True), portions_of(amount, rows * top, limit, skew, False)
    places = jnp.arange(amount)

    def named(lengths, offset_by):
        used = int((lengths > 0).sum())
        fixed = max(1, used // 4)
        passed = fixed + (places - fixed + offset_by * (used - fixed)) % max(1, amount - fixed)
        return jnp.zeros((amount,), jnp.int32).at[ranking[jnp.where(places < fixed, places, passed)]].set(jnp.asarray(lengths, jnp.int32))

    lengths = jnp.where(number % 4 == 0, named(crowded, number // 4), named(usual, number - number // 4 - 1))
    mixed = jax.random.permutation(jax.random.fold_in(own, 3), amount)
    giver, receiver = mixed[0:amount // 2 * 2:2], mixed[1:amount // 2 * 2:2]
    slack = jnp.minimum(lengths[giver] - 1, limit - lengths[receiver]) // 2
    slack = jnp.where((giver == ranking[0]) | (receiver == ranking[0]) | (lengths[receiver] == 0), 0, jnp.maximum(slack, 0))
    passed = jax.random.randint(jax.random.fold_in(own, 4), (amount // 2,), 0, 1 << 20) % (slack + 1)
    lengths = lengths.at[giver].add(-passed).at[receiver].add(passed)
    items = jnp.searchsorted(jnp.cumsum(lengths), jnp.arange(rows * top), side="right").astype(jnp.int32)
    grid = items.reshape(top, rows).T
    grid = grid[jax.random.permutation(jax.random.fold_in(own, 1), rows)]
    offset_by = jax.random.randint(jax.random.fold_in(own, 2), (rows, 1), 0, top)
    return jnp.take_along_axis(grid, (jnp.arange(top)[None, :] + offset_by) % top, axis=1)


def portions_of(amount, total, limit, slope, full):
    portions = [(1 << 20) // math.isqrt(grade ** slope) + 1 for grade in range(1, amount + 1)]
    largest = limit if full else min(limit, max(-(-total // amount), total * portions[0] // sum(portions)))
    least = 1 if total - largest >= amount - 1 else 0
    holding, rest = [largest] + [least] * (amount - 1), total - largest - least * (amount - 1)
    while rest > 0:
        free = [i for i in range(1, amount) if holding[i] < largest] or [i for i in range(1, amount) if holding[i] < limit]
        pool, left = sum([portions[i] for i in free]), rest
        for i in free:
            extra = min(limit - holding[i], max(1, left * portions[i] // pool), rest)
            holding[i] = holding[i] + extra
            rest = rest - extra
    return np.array(holding)


def centred(rng, shape, deviation, limit, cuts=(), kind=jnp.bfloat16):
    factor_of = levels(rng, shape, cuts, -0.22, 0.18) if cuts else 1.0
    drawn = jax.random.normal(rng, shape, jnp.float32) * deviation * factor_of
    return jnp.minimum(jnp.maximum(drawn, -limit), limit).astype(kind)


def setup_inputs(seed: int = 0, part: int = 0) -> dict:
    keys = jax.random.split(jax.random.key(seed), 15)
    own_keys = jax.random.split(jax.random.fold_in(keys[14], part), 15)
    features = centred(own_keys[0], (SCAN_ROWS, C), 1.0, 6.0, ((0, 16),))
    scan_order = jax.vmap(lambda own: jax.random.permutation(own, SCAN_DEV))(jax.random.split(own_keys[1], SCAN_DEVS)).reshape((SCAN_DEVS, SCAN_DEV)).astype(jnp.int32)
    kernel_map = draw_kernel_map(jax.random.fold_in(jax.random.fold_in(keys[14], part), 71), part)
    halo_send = draw_halo_send(jax.random.fold_in(jax.random.fold_in(keys[14], part), 71), part)
    down_route_keys = jax.random.split(jax.random.fold_in(own_keys[4], 1), (OWNERS * NB_OWN) // NB_OWN)
    down_route_turns = jax.random.permutation(jax.random.fold_in(own_keys[4], 3), (OWNERS * NB_OWN) // NB_OWN)
    down_route = jax.vmap(lambda own, number: shared_out(jax.random.fold_in(own_keys[4], 2), own, number, NB_OWN, OWNERS, 1, DCAP, 2))(down_route_keys, down_route_turns).reshape((OWNERS * NB_OWN, 1))
    conv1_weight = centred(keys[5], (K, C, C), (K * C) ** -0.5, 0.078125, ((1, 2),))
    conv2_weight = centred(keys[6], (K, C, C), (K * C) ** -0.5, 0.078125, ((1, 2),))
    down_weight = centred(keys[7], (8, C, C), (8 * C) ** -0.5, 0.125, ((1, 2),))
    gain_first = jnp.clip(1.0 + 0.18 * jax.random.normal(keys[8], (C,), jnp.float32), 0.1, 1.9)
    bias_first = centred(keys[9], (C,), 0.5, 3.0, ((0, 2),), jnp.float32)
    gain_second = jnp.clip(1.0 + 0.18 * jax.random.normal(keys[10], (C,), jnp.float32), 0.1, 1.9)
    bias_second = centred(keys[11], (C,), 0.5, 3.0, ((0, 2),), jnp.float32)
    gain_down = jnp.clip(1.0 + 0.18 * jax.random.normal(keys[12], (C,), jnp.float32), 0.1, 1.9)
    bias_down = centred(keys[13], (C,), 0.5, 3.0, ((0, 2),), jnp.float32)
    return {"features": features, "scan_order": scan_order, "kernel_map": kernel_map, "halo_send": halo_send, "down_route": down_route, "conv1_weight": conv1_weight, "conv2_weight": conv2_weight, "down_weight": down_weight, "gain_first": gain_first, "bias_first": bias_first, "gain_second": gain_second, "bias_second": bias_second, "gain_down": gain_down, "bias_down": bias_down}


def extend_blocks(blocks, halo_send):
    owners = blocks.shape[0]
    sends = halo_send.reshape(owners, 2, -1)
    upward = jax.vmap(lambda source, chosen: source[chosen])(blocks, sends[:, 0])
    downward = jax.vmap(lambda source, chosen: source[chosen])(blocks, sends[:, 1])
    zeros_rim = jnp.zeros_like(upward[:1])
    from_lower = jnp.concatenate([zeros_rim, upward[:-1]], axis=0)
    from_upper = jnp.concatenate([downward[1:], zeros_rim], axis=0)
    empty_block = jnp.zeros_like(blocks[:, :1])
    return jnp.concatenate([blocks, from_lower, from_upper, empty_block], axis=1)


def convolve(extended, weight, kernel_map):
    owners = extended.shape[0]
    tables = kernel_map.reshape(owners, -1, K)
    weight_wide = weight.astype(jnp.float32)
    offsets = jnp.arange(K, dtype=jnp.int32)[:, None]

    def one_owner(inputs):
        blocks, table = inputs
        product = jnp.einsum("brc,kdc->kbrd", blocks.astype(jnp.float32), weight_wide, precision=lax.Precision.HIGHEST)
        picked = product[offsets, table.T]
        return jnp.sum(picked, axis=0)

    return lax.map(one_owner, (extended, tables))


def reference(features, scan_order, kernel_map, halo_send, down_route, conv1_weight, conv2_weight, down_weight, gain_first, bias_first, gain_second, bias_second, gain_down, bias_down):
    owners = N_BRICK * N_SUB
    per_owner = SCAN_DEV // owners
    scan_grid = features.reshape(N_BRICK, N_CHAN, N_SUB, SCAN_DEV, C)
    orders = scan_order.reshape(N_BRICK, N_CHAN, N_SUB, SCAN_DEV, 1)
    ordered = jnp.take_along_axis(scan_grid, orders, axis=3)
    ordered = ordered.reshape(N_BRICK, N_CHAN, N_SUB, owners, per_owner, C)
    owner_rows = ordered.transpose(3, 0, 2, 1, 4, 5).reshape(owners, NB_OWN, BLK, C)
    conv_first = convolve(extend_blocks(owner_rows, halo_send), conv1_weight, kernel_map)
    hidden = jax.nn.relu(conv_first * gain_first + bias_first).astype(jnp.bfloat16)
    second = convolve(extend_blocks(hidden, halo_send), conv2_weight, kernel_map)
    refined = jax.nn.relu(second * gain_second + bias_second + owner_rows.astype(jnp.float32)).astype(jnp.bfloat16)
    children = refined.reshape(owners, NB_OWN, 8, 8, C).astype(jnp.float32)
    coarse = jnp.einsum("snoqi,oic->scnq", children, down_weight.astype(jnp.float32), precision=lax.Precision.HIGHEST)
    tile_values = jax.nn.relu(coarse * gain_down[:, None, None] + bias_down[:, None, None]).astype(jnp.bfloat16)
    destination = down_route.reshape(owners, NB_OWN)
    onehot = (destination[:, :, None] == jnp.arange(owners, dtype=jnp.int32)[None, None, :]).astype(jnp.int32)
    earlier = jnp.sum((jnp.cumsum(onehot, axis=1) - onehot) * onehot, axis=2)
    position = destination * DCAP + earlier
    selector = (position[:, None, :] == jnp.arange(owners * DCAP, dtype=jnp.int32)[None, :, None]).astype(jnp.float32)
    outgoing = jnp.einsum("spn,scnq->scpq", selector, tile_values.astype(jnp.float32), precision=lax.Precision.HIGHEST)
    outgoing = outgoing.reshape(owners, C, owners, DCAP * 8).transpose(2, 1, 0, 3)
    return outgoing.reshape(owners, C, owners * DCAP * 8).astype(jnp.bfloat16)
```

```python
import functools

import jax
import jax.numpy as jnp
from jax import lax
from jax.experimental import pallas as pl
from jax.experimental.pallas import tpu as pltpu
from jax.sharding import PartitionSpec as P

BLK = 64
CHILDREN = 8
F32 = jnp.float32
BF16 = jnp.bfloat16
NT = (((1,), (1,)), ((), ()))
NN = (((1,), (0,)), ((), ()))
VMEM = pl.BlockSpec(memory_space=pltpu.VMEM)
SMEM = pl.BlockSpec(memory_space=pltpu.SMEM)
LIMIT = pltpu.CompilerParams(vmem_limit_bytes=40 * 2**20)


def from_behind(block, axis, distance):
    devices = range(lax.axis_size(axis))
    route = [(i - distance, i) for i in devices if i - distance in devices]
    return lax.ppermute(block, axis, route)


def from_ahead(block, axis, distance):
    n = lax.axis_size(axis)
    return lax.ppermute(block, axis, [((i + distance) % n, i) for i in range(n)])


def to_ahead(block, axis, distance):
    n = lax.axis_size(axis)
    return lax.ppermute(block, axis, [(i, (i + distance) % n) for i in range(n)])


def sort_kernel(bricks, subs, place, order, rows, *outs):
    total = rows.shape[0]
    per = total // (bricks * subs)
    taken = lax.broadcasted_iota(jnp.int32, (total, total), 0) == order[...]
    onehot = jnp.where(taken, 1.0, 0.0).astype(BF16)
    picked = lax.dot_general(
        onehot, rows[...], (((0,), (0,)), ((), ())), preferred_element_type=F32
    ).astype(BF16)
    for b in range(bricks):
        for s in range(subs):
            away = lax.rem(s - place[1] + subs, subs)
            ahead = lax.rem(b - place[0] + bricks, bricks)
            start = (b * subs + s) * per
            for js in range(subs):

                @pl.when(away == js)
                def _(js=js, ahead=ahead, start=start):
                    outs[js][ahead] = picked[start : start + per]


def sort_rows(scan_order, features, place, bricks, subs):
    per = features.shape[0] // (bricks * subs)
    piece = jax.ShapeDtypeStruct((bricks, per, features.shape[1]), BF16)
    return pl.pallas_call(
        functools.partial(sort_kernel, bricks, subs),
        out_shape=[piece] * subs,
        in_specs=[SMEM, VMEM, VMEM],
        out_specs=[VMEM] * subs,
        compiler_params=LIMIT,
        name="sort_rows",
    )(place, scan_order, features)


def assemble_kernel(bricks, subs, chans, place, halo, *refs):
    parts, (rows, up, down) = refs[:-3], refs[-3:]
    split = BLK // parts[0].shape[1]
    for j in range(chans):
        chan = lax.rem(place[2] + j, chans)
        for jb in range(bricks):
            source = lax.rem(place[0] - jb + bricks, bricks)
            for js in range(subs):
                sub = lax.rem(place[1] + js, subs)
                rows[(source * subs + sub) * chans + chan] = parts[j * bricks + jb][js]
    for j in range(halo.shape[1]):
        up[pl.ds(j * split, split)] = rows[pl.ds(halo[0, j] * split, split)]
        down[pl.ds(j * split, split)] = rows[pl.ds(halo[1, j] * split, split)]


def assemble(parts, halo, place, bricks, subs, chans):
    per, channels = parts[0].shape[1:]
    pieces = bricks * subs * chans
    split = BLK // per
    sent = halo.shape[1] * split
    return pl.pallas_call(
        functools.partial(assemble_kernel, bricks, subs, chans),
        out_shape=[
            jax.ShapeDtypeStruct((count, per, channels), BF16) for count in (pieces, sent, sent)
        ],
        in_specs=[SMEM, SMEM] + [VMEM] * len(parts),
        out_specs=[VMEM] * 3,
        compiler_params=LIMIT,
        name="assemble",
    )(place, halo, *parts)


def block_sums(table, extended, weight, total):
    count = table.shape[0]
    group = min(count, 16)
    channels = extended.shape[2]

    def one_group(g, carry):
        first = g * group
        running = None
        for k in range(weight.shape[0]):
            picked = jnp.concatenate(
                [extended[table[first + n, k]] for n in range(group)], axis=0
            )
            product = lax.dot_general(picked, weight[k], NT, preferred_element_type=F32)
            running = product if running is None else running + product
        total[pl.ds(first, group)] = running.reshape(group, BLK, weight.shape[1])
        return carry

    if count == group:
        one_group(0, 0)
    else:
        lax.fori_loop(0, count // group, one_group, 0)


def first_kernel(table, halo, rows, lower, upper, weight, gain, bias, hidden, up, down, extended, total):
    count, reach = table.shape[0], halo.shape[1]
    extended[pl.ds(0, count)] = rows[...]
    extended[pl.ds(count, reach)] = lower[...]
    extended[pl.ds(count + reach, reach)] = upper[...]
    extended[count + 2 * reach] = jnp.zeros(extended.shape[1:], BF16)
    block_sums(table, extended, weight, total)
    value = total[...] * gain[...][None] + bias[...][None]
    hidden[...] = jnp.maximum(value, 0.0).astype(BF16)
    for j in range(reach):
        up[j] = hidden[halo[0, j]]
        down[j] = hidden[halo[1, j]]


def first_conv(table, halo, rows, lower, upper, weight, gain, bias):
    count, reach = table.shape[0], halo.shape[1]
    width, channels = weight.shape[1:]
    return pl.pallas_call(
        first_kernel,
        out_shape=[
            jax.ShapeDtypeStruct((n, BLK, width), BF16) for n in (count, reach, reach)
        ],
        in_specs=[SMEM, SMEM] + [VMEM] * 6,
        out_specs=[VMEM] * 3,
        scratch_shapes=[
            pltpu.VMEM((count + 2 * reach + 1, BLK, channels), BF16),
            pltpu.VMEM((count, BLK, width), F32),
        ],
        compiler_params=LIMIT,
        name="first_conv",
    )(table, halo, rows, lower, upper, weight, gain, bias)


def second_kernel(chans, table, place, rows, weight, down_weight, gain, bias, *refs):
    parts, (out, extended, total) = refs[:-3], refs[-3:]
    count = table.shape[0]
    width, channels = weight.shape[1:]
    reach = parts[1].shape[0]
    for j in range(chans):
        own, lower, upper = parts[3 * j : 3 * j + 3]
        for c in range(chans):

            @pl.when(lax.rem(place[2] + j, chans) == c)
            def _(own=own, lower=lower, upper=upper, c=c):
                lanes = slice(c * width, (c + 1) * width)
                extended[0:count, :, lanes] = own[...]
                extended[count : count + reach, :, lanes] = lower[...]
                extended[count + reach : count + 2 * reach, :, lanes] = upper[...]

    extended[count + 2 * reach] = jnp.zeros(extended.shape[1:], BF16)
    block_sums(table, extended, weight, total)
    for c in range(chans):

        @pl.when(place[2] == c)
        def _(c=c):
            total[...] = (
                total[...] * gain[...][None]
                + bias[...][None]
                + rows[:, :, c * width : (c + 1) * width].astype(F32)
            )

    refined = jnp.maximum(total[...], 0.0).reshape(count, CHILDREN, BLK // CHILDREN, width)
    cells = count * (BLK // CHILDREN)
    coarse = None
    for o in range(CHILDREN):
        child = refined[:, o].reshape(cells, width).astype(BF16)
        product = lax.dot_general(child, down_weight[o], NN, preferred_element_type=F32)
        coarse = product if coarse is None else coarse + product
    for c in range(chans):
        out[lax.rem(c - place[2] + chans, chans)] = coarse[
            :, c * width : (c + 1) * width
        ].astype(BF16)


def second_conv(table, place, rows, weight, down_weight, gain, bias, parts, chans):
    count = table.shape[0]
    reach = parts[1].shape[0]
    width, channels = weight.shape[1:]
    cells = count * (BLK // CHILDREN)
    return pl.pallas_call(
        functools.partial(second_kernel, chans),
        out_shape=jax.ShapeDtypeStruct((chans, cells, width), BF16),
        in_specs=[SMEM, SMEM] + [VMEM] * (5 + len(parts)),
        out_specs=VMEM,
        scratch_shapes=[
            pltpu.VMEM((count + 2 * reach + 1, BLK, channels), BF16),
            pltpu.VMEM((count, BLK, width), F32),
        ],
        compiler_params=LIMIT,
        name="second_conv",
    )(table, place, rows, weight, down_weight, gain, bias, *parts)


def tile_kernel(bricks, subs, capacity, route, place, gain, bias, *refs):
    owners = bricks * subs
    parts, outs, (slots, seen) = refs[: -subs - 2], refs[-subs - 2 : -2], refs[-2:]
    count = route.shape[0]
    coarse = parts[0][...].astype(F32)
    for part in parts[1:]:
        coarse = coarse + part[...].astype(F32)
    tiles = jnp.maximum(coarse * gain[...] + bias[...], 0.0)
    tiles = tiles.reshape(count, BLK // CHILDREN, tiles.shape[1])
    slots[...] = jnp.zeros(slots.shape, F32)
    for owner in range(owners):
        seen[owner] = 0
    for n in range(count):
        owner = route[n, 0]
        slot = seen[owner]
        seen[owner] = slot + 1
        slots[owner * capacity + slot] = tiles[n]
    for b in range(bricks):
        for s in range(subs):
            ahead = lax.rem(b - place[0] + bricks, bricks)
            away = lax.rem(s - place[1] + subs, subs)
            mine = slots[pl.ds((b * subs + s) * capacity, capacity)]
            mine = mine.reshape(capacity * (BLK // CHILDREN), mine.shape[2]).astype(BF16)
            for js in range(subs):

                @pl.when(away == js)
                def _(js=js, ahead=ahead, mine=mine):
                    outs[js][ahead] = mine


def coarse_tiles(route, place, gain, bias, parts, bricks, subs, capacity):
    width = gain.shape[1]
    per = BLK // CHILDREN
    piece = jax.ShapeDtypeStruct((bricks, capacity * per, width), BF16)
    return pl.pallas_call(
        functools.partial(tile_kernel, bricks, subs, capacity),
        out_shape=[piece] * subs,
        in_specs=[SMEM, SMEM] + [VMEM] * (2 + len(parts)),
        out_specs=[VMEM] * subs,
        scratch_shapes=[
            pltpu.VMEM((bricks * subs * capacity, per, width), F32),
            pltpu.SMEM((bricks * subs,), jnp.int32),
        ],
        compiler_params=LIMIT,
        name="coarse_tiles",
    )(route, place, gain, bias, *parts)


def arrive_kernel(bricks, subs, place, *refs):
    parts, out, held = refs[:-2], refs[-2], refs[-1]
    for jb in range(bricks):
        source = lax.rem(place[0] - jb + bricks, bricks)
        for js in range(subs):
            sub = lax.rem(place[1] + js, subs)
            held[source * subs + sub] = parts[jb][js].astype(F32)
    every = held[...].reshape(bricks * subs * held.shape[1], held.shape[2])
    out[0] = every.T.astype(BF16)


def arrived_tiles(place, parts, bricks, subs):
    slots, width = parts[0].shape[1:]
    return pl.pallas_call(
        functools.partial(arrive_kernel, bricks, subs),
        out_shape=jax.ShapeDtypeStruct((1, width, bricks * subs * slots), BF16),
        in_specs=[SMEM] + [VMEM] * len(parts),
        out_specs=VMEM,
        scratch_shapes=[pltpu.VMEM((bricks * subs, slots, width), F32)],
        compiler_params=LIMIT,
        name="arrived_tiles",
    )(place, *parts)


def to_owners(pieces, bricks, subs):
    by_sub = [pieces[0]]
    for js in range(1, subs):
        by_sub.append(to_ahead(pieces[subs - js], "sub", subs - js))
    stacked = [jnp.stack([piece[jb] for piece in by_sub]) for jb in range(bricks)]
    return [stacked[0]] + [to_ahead(stacked[jb], "brick", jb) for jb in range(1, bricks)]


def body(
    features,
    scan_order,
    kernel_map,
    halo_send,
    down_route,
    conv1_weight,
    conv2_weight,
    down_weight,
    gain_first,
    bias_first,
    gain_second,
    bias_second,
    gain_down,
    bias_down,
):
    bricks, subs, chans = (lax.axis_size(axis) for axis in ("brick", "sub", "chan"))
    owners = bricks * subs
    count, reach = kernel_map.shape[0], halo_send.shape[1]
    channels = features.shape[1]
    place = jnp.stack([lax.axis_index(axis) for axis in ("brick", "sub", "chan")])
    place = place.astype(jnp.int32)

    pieces = sort_rows(scan_order, features, place, bricks, subs)
    arrived = to_owners(pieces, bricks, subs)
    parts = arrived + [
        from_ahead(piece, "chan", j) for j in range(1, chans) for piece in arrived
    ]
    rows, up, down = assemble(parts, halo_send, place, bricks, subs, chans)
    lower = from_behind(up, ("brick", "sub"), 1)
    upper = from_behind(down, ("brick", "sub"), -1)
    rows = rows.reshape(count, BLK, channels)
    hidden, up, down = first_conv(
        kernel_map,
        halo_send,
        rows,
        lower.reshape(reach, BLK, channels),
        upper.reshape(reach, BLK, channels),
        conv1_weight,
        gain_first[None],
        bias_first[None],
    )
    lower = from_behind(up, ("brick", "sub"), 1)
    upper = from_behind(down, ("brick", "sub"), -1)
    parts = [hidden, lower, upper]
    for j in range(1, chans):
        parts += [from_ahead(part, "chan", j) for part in (hidden, lower, upper)]
    partial = second_conv(
        kernel_map,
        place,
        rows,
        conv2_weight,
        down_weight,
        gain_second[None],
        bias_second[None],
        parts,
        chans,
    )
    parts = [partial[0]] + [to_ahead(partial[j], "chan", j) for j in range(1, chans)]
    capacity = max(2, 2 * count // owners)
    pieces = coarse_tiles(
        down_route, place, gain_down[None], bias_down[None], parts, bricks, subs, capacity
    )
    return arrived_tiles(place, to_owners(pieces, bricks, subs), bricks, subs)


def solution(mesh):
    placed = (
        P(("groups", "brick", "chan", "sub"), None),
        P(("groups", "brick", "chan", "sub"), None),
        P(("groups", "brick", "sub"), None),
        P(("groups", "brick", "sub"), None),
        P(("groups", "brick", "sub"), None),
        P(None, "chan", None),
        P(None, "chan", None),
        P(None, "chan", None),
        P("chan"),
        P("chan"),
        P("chan"),
        P("chan"),
        P("chan"),
        P("chan"),
    )
    return jax.shard_map(
        body,
        mesh=mesh,
        in_specs=placed,
        out_specs=P(("groups", "brick", "sub"), "chan", None),
        check_vma=False,
    )
```

```python
import functools

import jax
import jax.numpy as jnp
from jax import lax
from jax.experimental import pallas as pl
from jax.experimental.pallas import tpu as pltpu
from jax.sharding import PartitionSpec as P

BLK = 64
CHILDREN = 8
CELLS = BLK // CHILDREN
ABSENT = -1e30
F32 = jnp.float32
BF16 = jnp.bfloat16
NT = (((1,), (1,)), ((), ()))
NN = (((1,), (0,)), ((), ()))
VMEM = pl.BlockSpec(memory_space=pltpu.VMEM)
SMEM = pl.BlockSpec(memory_space=pltpu.SMEM)
LIMIT = pltpu.CompilerParams(vmem_limit_bytes=40 * 2**20)


class Place:
    def __init__(self, ints, start, reach=0):
        self.ints, self.start, self.reach = ints, start, reach
        self.brick, self.sub, self.chan, self.parity = (ints[0, start + i] for i in range(4))

    def halo(self, direction, j):
        return self.ints[0, self.start + 4 + direction * self.reach + j]

    def route(self, n):
        return self.ints[0, self.start + 4 + 2 * self.reach + n]


def owner_pairs(block, parity, distance=0):
    bricks, subs, chans = (lax.axis_size(axis) for axis in ("brick", "sub", "chan"))

    def device(owner, chan):
        return (owner // subs * chans + chan % chans) * subs + owner % subs

    pairs = [(o, o + 1) for o in range(parity, bricks * subs - 1, 2)]
    pairs += [(b, a) for a, b in pairs]
    route = [(device(a, c + distance), device(b, c)) for a, b in pairs for c in range(chans)]
    return lax.ppermute(block, ("brick", "chan", "sub"), route)


def from_ahead(block, axis, distance):
    n = lax.axis_size(axis)
    return lax.ppermute(block, axis, [((i + distance) % n, i) for i in range(n)])


def to_ahead(block, axis, distance):
    n = lax.axis_size(axis)
    return lax.ppermute(block, axis, [(i, (i + distance) % n) for i in range(n)])


def sort_kernel(bricks, subs, ints, order, rows, *outs):
    total = rows.shape[0]
    place = Place(ints, total)
    per = total // (bricks * subs)
    taken = lax.broadcasted_iota(jnp.int32, (total, total), 0) == order[:, :total]
    onehot = jnp.where(taken, 1.0, 0.0).astype(BF16)
    picked = lax.dot_general(
        onehot, rows[...], (((0,), (0,)), ((), ())), preferred_element_type=F32
    ).astype(BF16)
    for b in range(bricks):
        for s in range(subs):
            away = lax.rem(s - place.sub + subs, subs)
            ahead = lax.rem(b - place.brick + bricks, bricks)
            start = (b * subs + s) * per
            for js in range(subs):

                @pl.when(away == js)
                def _(js=js, ahead=ahead, start=start):
                    outs[js][ahead] = picked[start : start + per]


def sort_rows(ints, features, bricks, subs):
    per = features.shape[0] // (bricks * subs)
    piece = jax.ShapeDtypeStruct((bricks, per, features.shape[1]), BF16)
    return pl.pallas_call(
        functools.partial(sort_kernel, bricks, subs),
        out_shape=[piece] * subs,
        in_specs=[SMEM, VMEM, VMEM],
        out_specs=[VMEM] * subs,
        compiler_params=LIMIT,
        name="sort_rows",
    )(ints, ints, features)


def assemble_kernel(start, reach, bricks, subs, chans, ints, *refs):
    parts, (rows, even, odd) = refs[:-3], refs[-3:]
    place = Place(ints, start, reach)
    split = BLK // parts[0].shape[1]
    for j in range(chans):
        chan = lax.rem(place.chan + j, chans)
        for jb in range(bricks):
            source = lax.rem(place.brick - jb + bricks, bricks)
            for js in range(subs):
                sub = lax.rem(place.sub + js, subs)
                rows[(source * subs + sub) * chans + chan] = parts[j * bricks + jb][js]
    for j in range(reach):
        even[pl.ds(j * split, split)] = rows[pl.ds(place.halo(place.parity, j) * split, split)]
        odd[pl.ds(j * split, split)] = rows[pl.ds(place.halo(1 - place.parity, j) * split, split)]


def assemble(ints, parts, start, reach, bricks, subs, chans):
    per, channels = parts[0].shape[1:]
    pieces = bricks * subs * chans
    split = BLK // per
    sent = reach * split
    return pl.pallas_call(
        functools.partial(assemble_kernel, start, reach, bricks, subs, chans),
        out_shape=[
            jax.ShapeDtypeStruct((count, per, channels), BF16) for count in (pieces, sent, sent)
        ],
        in_specs=[SMEM] + [VMEM] * len(parts),
        out_specs=[VMEM] * 3,
        compiler_params=LIMIT,
        name="assemble",
    )(ints, *parts)


def block_sums(table, blocks, weight, total):
    count = table.shape[0]
    group = min(count, 16)
    lanes = blocks.shape[2]
    offsets = weight.shape[2] // lanes

    def one_group(g, carry):
        first = g * group
        running = None
        for w in range(weight.shape[0]):
            inside = range(w * offsets, min((w + 1) * offsets, table.shape[1]))
            picked = jnp.concatenate(
                [
                    jnp.concatenate(
                        [blocks[jnp.minimum(table[first + n, k], count)] for k in inside], axis=1
                    )
                    for n in range(group)
                ],
                axis=0,
            )
            product = lax.dot_general(
                picked, weight[w, :, : len(inside) * lanes], NT, preferred_element_type=F32
            )
            running = product if running is None else running + product
        total[pl.ds(first, group)] = running.reshape(group, BLK, weight.shape[1])
        return carry

    if count == group:
        one_group(0, 0)
    else:
        lax.fori_loop(0, count // group, one_group, 0)


def rim_blocks(place, even, odd, lanes, rim):
    reach = even.shape[0]
    rim[pl.ds(reach * (1 - place.parity), reach), :, lanes] = even[...]
    rim[pl.ds(reach * place.parity, reach), :, lanes] = odd[...]


def rim_sums(count, table, rim, weight, products, total):
    blocks, offsets = rim.shape[0], table.shape[1]
    width, channels = weight.shape[1:]
    together = max(1, channels // width)
    rows = rim[...].reshape(blocks * BLK, channels)
    for k in range(0, offsets, together):
        size = min(together, offsets - k)
        product = lax.dot_general(
            rows,
            weight[k : k + size].reshape(size * width, channels),
            NT,
            preferred_element_type=F32,
        )
        for i in range(size):
            products[k + i, 0:blocks] = product[:, i * width : (i + 1) * width].reshape(
                blocks, BLK, width
            )
    products[:, blocks : blocks + 1] = jnp.zeros((offsets, 1, BLK, width), F32)

    def one_block(n, carry):
        running = total[n]
        for k in range(offsets):
            index = table[n, k]
            running = running + products[k, jnp.where(index < count, blocks, index - count)]
        total[n] = running
        return carry

    lax.fori_loop(0, count, one_block, 0, unroll=min(count, 16))


def cost(blocks, weight):
    offsets, width, channels = weight.shape
    return pl.CostEstimate(
        flops=4 * blocks * BLK * offsets * width * channels, bytes_accessed=0, transcendentals=0
    )


def own_first_kernel(table, rows, weight, total, blocks):
    count = rows.shape[0]
    blocks[0:count] = rows[...]
    blocks[count] = jnp.zeros(blocks.shape[1:], BF16)
    block_sums(table, blocks, weight, total)


def own_first(table, rows, weight):
    count, channels = rows.shape[0], rows.shape[2]
    return pl.pallas_call(
        own_first_kernel,
        out_shape=jax.ShapeDtypeStruct((count, BLK, weight.shape[1]), F32),
        in_specs=[SMEM, VMEM, VMEM],
        out_specs=VMEM,
        scratch_shapes=[pltpu.VMEM((count + 1, BLK, channels), BF16)],
        compiler_params=LIMIT,
        cost_estimate=cost(count, weight),
        name="own_first",
    )(table, rows, weight)


def rim_first_kernel(start, ints, table, vectors, own, even, odd, weight, hidden, even_out, odd_out, rim, products, total):
    count, reach = table.shape[0], even.shape[0]
    place = Place(ints, start, reach)
    rim_blocks(place, even, odd, slice(None), rim)
    total[...] = own[...]
    rim_sums(count, table, rim, weight, products, total)
    value = total[...] * vectors[0:1][None] + vectors[1:2][None]
    hidden[...] = jnp.maximum(value, 0.0).astype(BF16)
    for j in range(reach):
        even_out[j] = hidden[place.halo(place.parity, j)]
        odd_out[j] = hidden[place.halo(1 - place.parity, j)]


def rim_scratch(count, reach, weight):
    offsets, width, channels = weight.shape
    return [
        pltpu.VMEM((2 * reach, BLK, channels), BF16),
        pltpu.VMEM((offsets, 2 * reach + 1, BLK, width), F32),
        pltpu.VMEM((count, BLK, width), F32),
    ]


def rim_first(ints, table, vectors, own, even, odd, weight, start):
    count, reach, width = table.shape[0], even.shape[0], weight.shape[1]
    return pl.pallas_call(
        functools.partial(rim_first_kernel, start),
        out_shape=[
            jax.ShapeDtypeStruct((n, BLK, width), BF16) for n in (count, reach, reach)
        ],
        in_specs=[SMEM, SMEM] + [VMEM] * 5,
        out_specs=[VMEM] * 3,
        scratch_shapes=rim_scratch(count, reach, weight),
        compiler_params=LIMIT,
        cost_estimate=cost(2 * reach, weight),
        name="rim_first",
    )(ints, table, vectors, own, even, odd, weight)


def own_second_kernel(start, nearest, chans, ints, table, weight, *refs):
    parts, (total, blocks, beside) = refs[:-3], refs[-3:]
    count, width = parts[0].shape[0], parts[0].shape[2]
    place = Place(ints, start)
    lanes = blocks.shape[2]
    offsets = beside.shape[2] // lanes
    for i, part in enumerate(parts):
        blocks[0:count, :, i * width : (i + 1) * width] = part[...]
        for c in range(chans):

            @pl.when(lax.rem(place.chan + nearest + i, chans) == c)
            def _(i=i, c=c):
                for k in range(weight.shape[0]):
                    at = k % offsets * lanes + i * width
                    beside[k // offsets, :, at : at + width] = weight[
                        k, :, c * width : (c + 1) * width
                    ]

    blocks[count] = jnp.zeros(blocks.shape[1:], BF16)
    block_sums(table, blocks, beside, total)


def own_second(ints, table, weight, parts, start, nearest, chans):
    count, width = parts[0].shape[0], parts[0].shape[2]
    lanes = width * len(parts)
    offsets = max(1, weight.shape[2] // lanes)
    groups = -(-weight.shape[0] // offsets)
    return pl.pallas_call(
        functools.partial(own_second_kernel, start, nearest, chans),
        out_shape=jax.ShapeDtypeStruct((count, BLK, width), F32),
        in_specs=[SMEM, SMEM] + [VMEM] * (1 + len(parts)),
        out_specs=VMEM,
        scratch_shapes=[
            pltpu.VMEM((count + 1, BLK, lanes), BF16),
            pltpu.VMEM((groups, width, lanes * offsets), BF16),
        ],
        compiler_params=LIMIT,
        cost_estimate=cost(count // 2, weight),
        name="own_second",
    )(ints, table, weight, *parts)


def rim_second_kernel(start, bricks, subs, chans, owns, ints, table, vectors, rows, weight, down_weight, *refs):
    (even, odd), refs = refs[:2], refs[2:]
    sums, refs = refs[:owns], refs[owns:]
    fars, (out, rim, products, total, slots, seen) = refs[:-6], refs[-6:]
    count, reach = table.shape[0], even.shape[0]
    width = weight.shape[1]
    place = Place(ints, start, reach)
    for j in range(chans):
        near = (even, odd) if j == 0 else (fars[j - 1].at[0:reach], fars[j - 1].at[reach:])
        for c in range(chans):

            @pl.when(lax.rem(place.chan + j, chans) == c)
            def _(near=near, c=c):
                rim_blocks(place, *near, slice(c * width, (c + 1) * width), rim)

    total[...] = sums[0][...]
    for more in sums[1:]:
        total[...] += more[...]
    rim_sums(count, table, rim, weight, products, total)
    for c in range(chans):

        @pl.when(place.chan == c)
        def _(c=c):
            total[...] = (
                total[...] * vectors[2:3][None]
                + vectors[3:4][None]
                + rows[:, :, c * width : (c + 1) * width].astype(F32)
            )

    refined = jnp.maximum(total[...], 0.0).reshape(count, CHILDREN, CELLS, width)
    coarse = None
    for o in range(CHILDREN):
        child = refined[:, o].reshape(count * CELLS, width).astype(BF16)
        product = lax.dot_general(child, down_weight[o], NN, preferred_element_type=F32)
        coarse = product if coarse is None else coarse + product
    slots[...] = jnp.full(slots.shape, ABSENT, F32)
    for owner in range(bricks * subs):
        seen[owner] = 0
    for n in range(count):
        owner = place.route(n)
        slot = seen[owner]
        seen[owner] = slot + 1
        device = owner // subs * (chans * subs) + lax.rem(owner, subs)
        for c in range(chans):
            slots[device + c * subs, pl.ds(pl.multiple_of(slot * CELLS, CELLS), CELLS)] = coarse[
                n * CELLS : (n + 1) * CELLS, c * width : (c + 1) * width
            ]
    out[...] = slots[...].astype(BF16)


def rim_second(ints, table, vectors, rows, weight, down_weight, even, odd, sums, fars, start, bricks, subs, chans, capacity):
    count, reach, width = table.shape[0], even.shape[0], weight.shape[1]
    slots = (bricks * subs * chans, capacity * CELLS, width)
    return pl.pallas_call(
        functools.partial(rim_second_kernel, start, bricks, subs, chans, len(sums)),
        out_shape=jax.ShapeDtypeStruct(slots, BF16),
        in_specs=[SMEM, SMEM] + [VMEM] * (6 + len(sums) + len(fars)),
        out_specs=VMEM,
        scratch_shapes=rim_scratch(count, reach, weight)
        + [pltpu.VMEM(slots, F32), pltpu.SMEM((bricks * subs,), jnp.int32)],
        compiler_params=LIMIT,
        cost_estimate=cost(2 * reach, weight),
        name="rim_second",
    )(ints, table, vectors, rows, weight, down_weight, even, odd, *sums, *fars)


def arrive_kernel(bricks, subs, chans, vectors, parts, out):
    held = []
    for b in range(bricks):
        for s in range(subs):
            coarse = None
            for c in range(chans):
                part = parts[(b * chans + c) * subs + s].astype(F32)
                coarse = part if coarse is None else coarse + part
            held.append(coarse)
    coarse = jnp.concatenate(held, axis=0)
    tiles = jnp.maximum(coarse * vectors[4:5] + vectors[5:6], 0.0)
    tiles = jnp.where(coarse < ABSENT / 2, 0.0, tiles)
    out[0] = tiles.T.astype(BF16)


def arrived_tiles(vectors, parts, bricks, subs, chans):
    slots, width = parts.shape[1:]
    return pl.pallas_call(
        functools.partial(arrive_kernel, bricks, subs, chans),
        out_shape=jax.ShapeDtypeStruct((1, width, bricks * subs * slots), BF16),
        in_specs=[VMEM, VMEM],
        out_specs=VMEM,
        compiler_params=LIMIT,
        name="arrived_tiles",
    )(vectors, parts)


def to_owners(pieces, bricks, subs):
    by_sub = [pieces[0]]
    for js in range(1, subs):
        by_sub.append(to_ahead(pieces[subs - js], "sub", subs - js))
    stacked = [jnp.stack([piece[jb] for piece in by_sub]) for jb in range(bricks)]
    return [stacked[0]] + [to_ahead(stacked[jb], "brick", jb) for jb in range(1, bricks)]


def body(
    features,
    scan_order,
    kernel_map,
    halo_send,
    down_route,
    conv1_weight,
    conv2_weight,
    down_weight,
    gain_first,
    bias_first,
    gain_second,
    bias_second,
    gain_down,
    bias_down,
):
    bricks, subs, chans = (lax.axis_size(axis) for axis in ("brick", "sub", "chan"))
    owners = bricks * subs
    count, reach = kernel_map.shape[0], halo_send.shape[1]
    channels = features.shape[1]
    start = features.shape[0]
    brick, sub, chan = (lax.axis_index(axis) for axis in ("brick", "sub", "chan"))
    place = jnp.stack([brick, sub, chan, lax.rem(brick * subs + sub, 2)]).astype(jnp.int32)
    ints = jnp.concatenate(
        [scan_order, place[None], halo_send.reshape(1, -1), down_route.reshape(1, -1)], axis=1
    )
    vectors = jnp.stack(
        [gain_first, bias_first, gain_second, bias_second, gain_down, bias_down]
    )
    pieces = sort_rows(ints, features, bricks, subs)
    arrived = to_owners(pieces, bricks, subs)
    parts = arrived + [
        from_ahead(piece, "chan", j) for j in range(1, chans) for piece in arrived
    ]
    rows, even, odd = assemble(ints, parts, start, reach, bricks, subs, chans)
    rows = rows.reshape(count, BLK, channels)
    even = owner_pairs(even, 0).reshape(reach, BLK, channels)
    odd = owner_pairs(odd, 1).reshape(reach, BLK, channels)
    own = own_first(kernel_map, rows, conv1_weight)
    hidden, even, odd = rim_first(
        ints, kernel_map, vectors, own, even, odd, conv1_weight, start
    )
    others = [from_ahead(hidden, "chan", j) for j in range(1, chans)]
    even, odd = owner_pairs(even, 0), owner_pairs(odd, 1)
    rim = jnp.concatenate([even, odd], axis=0)
    fars = [from_ahead(rim, "chan", j) for j in range(1, chans)]
    sums = [own_second(ints, kernel_map, conv2_weight, [hidden], start, 0, chans)]
    if others:
        sums.append(own_second(ints, kernel_map, conv2_weight, others, start, 1, chans))
    capacity = max(2, 2 * count // owners)
    partial = rim_second(
        ints,
        kernel_map,
        vectors,
        rows,
        conv2_weight,
        down_weight,
        even,
        odd,
        sums,
        fars,
        start,
        bricks,
        subs,
        chans,
        capacity,
    )
    partial = lax.all_to_all(
        partial, ("brick", "chan", "sub"), split_axis=0, concat_axis=0, tiled=True
    )
    return arrived_tiles(vectors, partial, bricks, subs, chans)


def solution(mesh):
    placed = (
        P(("groups", "brick", "chan", "sub"), None),
        P(("groups", "brick", "chan", "sub"), None),
        P(("groups", "brick", "sub"), None),
        P(("groups", "brick", "sub"), None),
        P(("groups", "brick", "sub"), None),
        P(None, "chan", None),
        P(None, "chan", None),
        P(None, "chan", None),
        P("chan"),
        P("chan"),
        P("chan"),
        P("chan"),
        P("chan"),
        P("chan"),
    )
    return jax.shard_map(
        body,
        mesh=mesh,
        in_specs=placed,
        out_specs=P(("groups", "brick", "sub"), "chan", None),
        check_vma=False,
    )
```

```python
import functools

import jax
import jax.numpy as jnp
from jax import lax
from jax.experimental import pallas as pl
from jax.experimental.pallas import tpu as pltpu
from jax.sharding import PartitionSpec as P

BLK = 64
CHILDREN = 8
CELLS = BLK // CHILDREN
ABSENT = -1e30
F32 = jnp.float32
BF16 = jnp.bfloat16
NT = (((1,), (1,)), ((), ()))
NN = (((1,), (0,)), ((), ()))
VMEM = pl.BlockSpec(memory_space=pltpu.VMEM)
SMEM = pl.BlockSpec(memory_space=pltpu.SMEM)
LIMIT = pltpu.CompilerParams(vmem_limit_bytes=40 * 2**20)


class Place:
    def __init__(self, ints, start, reach=0):
        self.ints, self.start, self.reach = ints, start, reach
        self.brick, self.sub, self.chan, self.parity = (ints[0, start + i] for i in range(4))

    def halo(self, direction, j):
        return self.ints[0, self.start + 4 + direction * self.reach + j]

    def route(self, n):
        return self.ints[0, self.start + 4 + 2 * self.reach + n]


def owner_pairs(block, parity, distance=0):
    bricks, subs, chans = (lax.axis_size(axis) for axis in ("brick", "sub", "chan"))

    def device(owner, chan):
        return (owner // subs * chans + chan % chans) * subs + owner % subs

    pairs = [(o, o + 1) for o in range(parity, bricks * subs - 1, 2)]
    pairs += [(b, a) for a, b in pairs]
    route = [(device(a, c + distance), device(b, c)) for a, b in pairs for c in range(chans)]
    return lax.ppermute(block, ("brick", "chan", "sub"), route)


def from_ahead(block, axis, distance):
    n = lax.axis_size(axis)
    return lax.ppermute(block, axis, [((i + distance) % n, i) for i in range(n)])


def to_ahead(block, axis, distance):
    n = lax.axis_size(axis)
    return lax.ppermute(block, axis, [(i, (i + distance) % n) for i in range(n)])


def sorted_rows(scan_order, features):
    total = features.shape[0]
    taken = scan_order.reshape(total, 1) == jnp.arange(total, dtype=jnp.int32)[None]
    return jnp.dot(taken.astype(BF16), features, preferred_element_type=F32).astype(BF16)


def assemble_kernel(start, reach, bricks, subs, chans, keys, ints, *refs):
    parts, (rows, even, odd) = dict(zip(keys, refs[:-3])), refs[-3:]
    place = Place(ints, start, reach)
    split = BLK // parts[0, 0].shape[1]
    for (jb, j), part in parts.items():
        source = lax.rem(place.brick - jb + bricks, bricks)
        chan = lax.rem(place.chan + j, chans)
        for js in range(subs):
            sub = lax.rem(place.sub + js, subs)
            rows[(source * subs + sub) * chans + chan] = part[js]
    for j in range(reach):
        even[pl.ds(j * split, split)] = rows[pl.ds(place.halo(place.parity, j) * split, split)]
        odd[pl.ds(j * split, split)] = rows[pl.ds(place.halo(1 - place.parity, j) * split, split)]


def assemble(ints, parts, start, reach, bricks, subs, chans):
    per, channels = parts[0, 0].shape[1:]
    pieces = bricks * subs * chans
    split = BLK // per
    sent = reach * split
    return pl.pallas_call(
        functools.partial(assemble_kernel, start, reach, bricks, subs, chans, tuple(parts)),
        out_shape=[
            jax.ShapeDtypeStruct((count, per, channels), BF16) for count in (pieces, sent, sent)
        ],
        in_specs=[SMEM] + [VMEM] * len(parts),
        out_specs=[VMEM] * 3,
        compiler_params=LIMIT,
        name="assemble",
    )(ints, *parts.values())


def block_sums(table, blocks, weight, total):
    count = table.shape[0]
    group = min(count, 16)
    lanes = blocks.shape[2]
    offsets = weight.shape[2] // lanes

    def one_group(g, carry):
        first = g * group
        running = None
        for w in range(weight.shape[0]):
            inside = range(w * offsets, min((w + 1) * offsets, table.shape[1]))
            picked = jnp.concatenate(
                [
                    jnp.concatenate(
                        [blocks[jnp.minimum(table[first + n, k], count)] for k in inside], axis=1
                    )
                    for n in range(group)
                ],
                axis=0,
            )
            product = lax.dot_general(
                picked, weight[w, :, : len(inside) * lanes], NT, preferred_element_type=F32
            )
            running = product if running is None else running + product
        total[pl.ds(first, group)] = running.reshape(group, BLK, weight.shape[1])
        return carry

    if count == group:
        one_group(0, 0)
    else:
        lax.fori_loop(0, count // group, one_group, 0)


def rim_blocks(place, even, odd, lanes, rim):
    reach = even.shape[0]
    rim[pl.ds(reach * (1 - place.parity), reach), :, lanes] = even[...]
    rim[pl.ds(reach * place.parity, reach), :, lanes] = odd[...]


def named_sums(table, given, weight, products, total):
    blocks, offsets = given.shape[0], table.shape[1]
    width, channels = weight.shape[1:]
    together = max(1, channels // width)
    rows = given[...].reshape(blocks * BLK, channels)
    for k in range(0, offsets, together):
        size = min(together, offsets - k)
        product = lax.dot_general(
            rows,
            weight[k : k + size].reshape(size * width, channels),
            NT,
            preferred_element_type=F32,
        )
        for i in range(size):
            products[k + i, 0:blocks] = product[:, i * width : (i + 1) * width].reshape(
                blocks, BLK, width
            )
    products[:, blocks : blocks + 1] = jnp.zeros((offsets, 1, BLK, width), F32)

    def one_block(n, carry):
        running = total[n]
        for k in range(offsets):
            running = running + products[k, table[n, k]]
        total[n] = running
        return carry

    lax.fori_loop(0, table.shape[0], one_block, 0, unroll=min(table.shape[0], 16))


def cost(blocks, weight):
    offsets, width, channels = weight.shape
    return pl.CostEstimate(
        flops=4 * blocks * BLK * offsets * width * channels, bytes_accessed=0, transcendentals=0
    )


def own_first_kernel(table, rows, weight, total, blocks):
    count = rows.shape[0]
    blocks[0:count] = rows[...]
    blocks[count] = jnp.zeros(blocks.shape[1:], BF16)
    block_sums(table, blocks, weight, total)


def own_first(table, rows, weight):
    count, channels = rows.shape[0], rows.shape[2]
    return pl.pallas_call(
        own_first_kernel,
        out_shape=jax.ShapeDtypeStruct((count, BLK, weight.shape[1]), F32),
        in_specs=[SMEM, VMEM, VMEM],
        out_specs=VMEM,
        scratch_shapes=[pltpu.VMEM((count + 1, BLK, channels), BF16)],
        compiler_params=LIMIT,
        cost_estimate=cost(count, weight),
        name="own_first",
    )(table, rows, weight)


def pieces_first_kernel(bricks, subs, behind, started, ints, table, weight, *refs):
    parts, (total, held, products) = refs[:-3], refs[-3:]
    if started:
        parts, before = parts[:-1], parts[-1]
    place = Place(ints, 0)
    for jb, part in zip(behind, parts):
        source = lax.rem(place.brick - jb + bricks, bricks)
        for js in range(subs):
            held[source * subs + lax.rem(place.sub + js, subs)] = part[js]
    total[...] = before[...] if started else jnp.zeros(total.shape, F32)
    named_sums(table, held, weight, products, total)


def pieces_first(ints, table, weight, parts, before, j, bricks, subs):
    offsets, width, channels = weight.shape
    sums = jax.ShapeDtypeStruct((table.shape[0], BLK, width), F32)
    held = bricks * subs
    behind = tuple(jb for jb, far in parts if far == j)
    given = [parts[jb, j] for jb in behind] + ([] if before is None else [before])
    return pl.pallas_call(
        functools.partial(pieces_first_kernel, bricks, subs, behind, before is not None),
        out_shape=sums,
        in_specs=[SMEM, SMEM] + [VMEM] * (1 + len(given)),
        out_specs=VMEM,
        scratch_shapes=[
            pltpu.VMEM((held, BLK, channels), BF16),
            pltpu.VMEM((offsets, held + 1, BLK, width), F32),
        ],
        compiler_params=LIMIT,
        cost_estimate=cost(held, weight),
        name="pieces_first",
    )(ints, table, weight, *given)


def rim_first_kernel(start, ints, table, vectors, own, even, odd, weight, hidden, even_out, odd_out, rim, products, total):
    count, reach = table.shape[0], even.shape[0]
    place = Place(ints, start, reach)
    rim_blocks(place, even, odd, slice(None), rim)
    total[...] = own[...]
    named_sums(table, rim, weight, products, total)
    value = total[...] * vectors[0:1][None] + vectors[1:2][None]
    hidden[...] = jnp.maximum(value, 0.0).astype(BF16)
    for j in range(reach):
        even_out[j] = hidden[place.halo(place.parity, j)]
        odd_out[j] = hidden[place.halo(1 - place.parity, j)]


def rim_scratch(count, reach, weight):
    offsets, width, channels = weight.shape
    return [
        pltpu.VMEM((2 * reach, BLK, channels), BF16),
        pltpu.VMEM((offsets, 2 * reach + 1, BLK, width), F32),
        pltpu.VMEM((count, BLK, width), F32),
    ]


def rim_first(ints, table, vectors, own, even, odd, weight, start):
    count, reach, width = table.shape[0], even.shape[0], weight.shape[1]
    return pl.pallas_call(
        functools.partial(rim_first_kernel, start),
        out_shape=[
            jax.ShapeDtypeStruct((n, BLK, width), BF16) for n in (count, reach, reach)
        ],
        in_specs=[SMEM, SMEM] + [VMEM] * 5,
        out_specs=[VMEM] * 3,
        scratch_shapes=rim_scratch(count, reach, weight),
        compiler_params=LIMIT,
        cost_estimate=cost(2 * reach, weight),
        name="rim_first",
    )(ints, table, vectors, own, even, odd, weight)


def pack_kernel(even, odd, *refs):
    out = refs[-1]
    out[0 : even.shape[0]] = even[...]
    out[even.shape[0] :] = odd[...]


def pack(even, odd, after):
    return pl.pallas_call(
        pack_kernel,
        out_shape=jax.ShapeDtypeStruct((2 * even.shape[0],) + even.shape[1:], BF16),
        in_specs=[VMEM, VMEM] + [pl.BlockSpec(memory_space=pl.ANY)] * len(after),
        out_specs=VMEM,
        compiler_params=LIMIT,
        name="pack",
    )(even, odd, *after)


def own_second_kernel(start, nearest, chans, ints, table, weight, *refs):
    parts, (total, blocks, beside) = refs[:-3], refs[-3:]
    count, width = parts[0].shape[0], parts[0].shape[2]
    place = Place(ints, start)
    lanes = blocks.shape[2]
    offsets = beside.shape[2] // lanes
    for i, part in enumerate(parts):
        blocks[0:count, :, i * width : (i + 1) * width] = part[...]
        for c in range(chans):

            @pl.when(lax.rem(place.chan + nearest + i, chans) == c)
            def _(i=i, c=c):
                for k in range(weight.shape[0]):
                    at = k % offsets * lanes + i * width
                    beside[k // offsets, :, at : at + width] = weight[
                        k, :, c * width : (c + 1) * width
                    ]

    blocks[count] = jnp.zeros(blocks.shape[1:], BF16)
    block_sums(table, blocks, beside, total)


def own_second(ints, table, weight, parts, start, nearest, chans):
    count, width = parts[0].shape[0], parts[0].shape[2]
    lanes = width * len(parts)
    offsets = max(1, weight.shape[2] // lanes)
    groups = -(-weight.shape[0] // offsets)
    return pl.pallas_call(
        functools.partial(own_second_kernel, start, nearest, chans),
        out_shape=jax.ShapeDtypeStruct((count, BLK, width), F32),
        in_specs=[SMEM, SMEM] + [VMEM] * (1 + len(parts)),
        out_specs=VMEM,
        scratch_shapes=[
            pltpu.VMEM((count + 1, BLK, lanes), BF16),
            pltpu.VMEM((groups, width, lanes * offsets), BF16),
        ],
        compiler_params=LIMIT,
        cost_estimate=cost(count // 2, weight),
        name="own_second",
    )(ints, table, weight, *parts)


def rim_second_kernel(start, bricks, subs, chans, owns, ints, table, vectors, rows, weight, down_weight, *refs):
    (even, odd), refs = refs[:2], refs[2:]
    sums, refs = refs[:owns], refs[owns:]
    fars, (out, rim, products, total, slots, seen) = refs[:-6], refs[-6:]
    count, reach = table.shape[0], even.shape[0]
    width = weight.shape[1]
    place = Place(ints, start, reach)
    for j in range(chans):
        near = (even, odd) if j == 0 else (fars[j - 1].at[0:reach], fars[j - 1].at[reach:])
        for c in range(chans):

            @pl.when(lax.rem(place.chan + j, chans) == c)
            def _(near=near, c=c):
                rim_blocks(place, *near, slice(c * width, (c + 1) * width), rim)

    total[...] = sums[0][...]
    for more in sums[1:]:
        total[...] += more[...]
    named_sums(table, rim, weight, products, total)
    for c in range(chans):

        @pl.when(place.chan == c)
        def _(c=c):
            total[...] = (
                total[...] * vectors[2:3][None]
                + vectors[3:4][None]
                + rows[:, :, c * width : (c + 1) * width].astype(F32)
            )

    refined = jnp.maximum(total[...], 0.0).reshape(count, CHILDREN, CELLS, width)
    coarse = None
    for o in range(CHILDREN):
        child = refined[:, o].reshape(count * CELLS, width).astype(BF16)
        product = lax.dot_general(child, down_weight[o], NN, preferred_element_type=F32)
        coarse = product if coarse is None else coarse + product
    slots[...] = jnp.full(slots.shape, ABSENT, F32)
    for owner in range(bricks * subs):
        seen[owner] = 0
    for n in range(count):
        owner = place.route(n)
        slot = seen[owner]
        seen[owner] = slot + 1
        device = owner // subs * (chans * subs) + lax.rem(owner, subs)
        for c in range(chans):
            slots[device + c * subs, pl.ds(pl.multiple_of(slot * CELLS, CELLS), CELLS)] = coarse[
                n * CELLS : (n + 1) * CELLS, c * width : (c + 1) * width
            ]
    out[...] = slots[...].astype(BF16)


def rim_second(ints, table, vectors, rows, weight, down_weight, even, odd, sums, fars, start, bricks, subs, chans, capacity):
    count, reach, width = table.shape[0], even.shape[0], weight.shape[1]
    slots = (bricks * subs * chans, capacity * CELLS, width)
    return pl.pallas_call(
        functools.partial(rim_second_kernel, start, bricks, subs, chans, len(sums)),
        out_shape=jax.ShapeDtypeStruct(slots, BF16),
        in_specs=[SMEM, SMEM] + [VMEM] * (6 + len(sums) + len(fars)),
        out_specs=VMEM,
        scratch_shapes=rim_scratch(count, reach, weight)
        + [pltpu.VMEM(slots, F32), pltpu.SMEM((bricks * subs,), jnp.int32)],
        compiler_params=LIMIT,
        cost_estimate=cost(2 * reach, weight),
        name="rim_second",
    )(ints, table, vectors, rows, weight, down_weight, even, odd, *sums, *fars)


def arrive_kernel(bricks, subs, chans, vectors, parts, out):
    held = []
    for b in range(bricks):
        for s in range(subs):
            coarse = None
            for c in range(chans):
                part = parts[(b * chans + c) * subs + s].astype(F32)
                coarse = part if coarse is None else coarse + part
            held.append(coarse)
    coarse = jnp.concatenate(held, axis=0)
    tiles = jnp.maximum(coarse * vectors[4:5] + vectors[5:6], 0.0)
    tiles = jnp.where(coarse < ABSENT / 2, 0.0, tiles)
    out[0] = tiles.T.astype(BF16)


def arrived_tiles(vectors, parts, bricks, subs, chans):
    slots, width = parts.shape[1:]
    return pl.pallas_call(
        functools.partial(arrive_kernel, bricks, subs, chans),
        out_shape=jax.ShapeDtypeStruct((1, width, bricks * subs * slots), BF16),
        in_specs=[VMEM, VMEM],
        out_specs=VMEM,
        compiler_params=LIMIT,
        name="arrived_tiles",
    )(vectors, parts)


def to_owners(ordered, chans):
    bricks, subs = ordered.shape[:2]
    brick, sub = lax.axis_index("brick"), lax.axis_index("sub")

    def pieces(js):
        column = lax.dynamic_index_in_dim(ordered, lax.rem(sub + js, subs), 1, keepdims=False)
        doubled = jnp.concatenate([column, column], axis=0)
        return lax.dynamic_slice_in_dim(doubled, brick, bricks, 0)

    by_sub = [pieces(0)]
    for js in range(1, subs):
        by_sub.append(to_ahead(pieces(subs - js), "sub", subs - js))
    stacked = [jnp.stack([piece[jb] for piece in by_sub]) for jb in range(bricks)]
    order = sorted(range(1, bricks), key=lambda jb: min(jb, bricks - jb))
    parts = {(0, 0): stacked[0]}
    for jb in order:
        parts[jb, 0] = to_ahead(stacked[jb], "brick", jb)
    for jb in [0] + order:
        for j in range(1, chans):
            parts[jb, j] = from_ahead(parts[jb, 0], "chan", j)
    return parts


def body(
    features,
    scan_order,
    kernel_map,
    halo_send,
    down_route,
    conv1_weight,
    conv2_weight,
    down_weight,
    gain_first,
    bias_first,
    gain_second,
    bias_second,
    gain_down,
    bias_down,
):
    bricks, subs, chans = (lax.axis_size(axis) for axis in ("brick", "sub", "chan"))
    owners = bricks * subs
    count, reach = kernel_map.shape[0], halo_send.shape[1]
    channels = features.shape[1]
    start = 0
    brick, sub, chan = (lax.axis_index(axis) for axis in ("brick", "sub", "chan"))
    place = jnp.stack([brick, sub, chan, lax.rem(brick * subs + sub, 2)]).astype(jnp.int32)
    ordered = sorted_rows(scan_order, features)
    ordered = ordered.reshape(bricks, subs, features.shape[0] // owners, channels)
    parts = to_owners(ordered, chans)
    ints = jnp.concatenate(
        [place[None], halo_send[0:1], halo_send[1:2], down_route.reshape(1, -1)], axis=1
    )
    vectors = jnp.stack(
        [gain_first, bias_first, gain_second, bias_second, gain_down, bias_down]
    )
    rows, even, odd = assemble(ints, parts, start, reach, bricks, subs, chans)
    rows = rows.reshape(count, BLK, channels)
    even = owner_pairs(even, 0).reshape(reach, BLK, channels)
    odd = owner_pairs(odd, 1).reshape(reach, BLK, channels)
    outside = jnp.where(kernel_map < count, 2 * reach, kernel_map - count)
    if features.shape[0] // owners == BLK:
        own = None
        for j in range(chans):
            here = (kernel_map < count) & (lax.rem(kernel_map, chans) == lax.rem(chan + j, chans))
            inside = jnp.where(here, lax.div(kernel_map, chans), owners)
            own = pieces_first(ints, inside, conv1_weight, parts, own, j, bricks, subs)
    else:
        own = own_first(kernel_map, rows, conv1_weight)
    hidden, even, odd = rim_first(
        ints, outside, vectors, own, even, odd, conv1_weight, start
    )
    others = [from_ahead(hidden, "chan", j) for j in range(1, chans)]
    even, odd = owner_pairs(even, 0), owner_pairs(odd, 1)
    rim = pack(even, odd, others)
    fars = [from_ahead(rim, "chan", j) for j in range(1, chans)]
    sums = [own_second(ints, kernel_map, conv2_weight, [hidden], start, 0, chans)]
    if others:
        sums.append(own_second(ints, kernel_map, conv2_weight, others, start, 1, chans))
    capacity = max(2, 2 * count // owners)
    partial = rim_second(
        ints,
        outside,
        vectors,
        rows,
        conv2_weight,
        down_weight,
        even,
        odd,
        sums,
        fars,
        start,
        bricks,
        subs,
        chans,
        capacity,
    )
    partial = lax.all_to_all(
        partial, ("brick", "chan", "sub"), split_axis=0, concat_axis=0, tiled=True
    )
    return arrived_tiles(vectors, partial, bricks, subs, chans)


def solution(mesh):
    placed = (
        P(("groups", "brick", "chan", "sub"), None),
        P(("groups", "brick", "chan", "sub"), None),
        P(("groups", "brick", "sub"), None),
        P(("groups", "brick", "sub"), None),
        P(("groups", "brick", "sub"), None),
        P(None, "chan", None),
        P(None, "chan", None),
        P(None, "chan", None),
        P("chan"),
        P("chan"),
        P("chan"),
        P("chan"),
        P("chan"),
        P("chan"),
    )
    return jax.shard_map(
        body,
        mesh=mesh,
        in_specs=placed,
        out_specs=P(("groups", "brick", "sub"), "chan", None),
        check_vma=False,
    )
```

```python
import functools

import jax
import jax.numpy as jnp
from jax import lax
from jax.experimental import pallas as pl
from jax.experimental.pallas import tpu as pltpu
from jax.sharding import PartitionSpec as P

BLK = 64
CHILDREN = 8
CELLS = BLK // CHILDREN
ABSENT = -1e30
F32 = jnp.float32
BF16 = jnp.bfloat16
NT = (((1,), (1,)), ((), ()))
NN = (((1,), (0,)), ((), ()))
VMEM = pl.BlockSpec(memory_space=pltpu.VMEM)
LIMIT = pltpu.CompilerParams(vmem_limit_bytes=40 * 2**20)


class Place:
    def __init__(self):
        self.brick, self.sub, self.chan = (lax.axis_index(a) for a in ("brick", "sub", "chan"))
        self.parity = lax.rem(self.brick * lax.axis_size("sub") + self.sub, 2)


class Scalars:
    def __init__(self, given, held, semaphore):
        self.copies = [
            pltpu.make_async_copy(source, target, semaphore.at[i])
            for i, (source, target) in enumerate(zip(given, held))
        ]
        for copy in self.copies:
            copy.start()

    def wait(self):
        for copy in self.copies:
            copy.wait()


def scalar_scratch(*arrays):
    return [pltpu.SMEM(x.shape, jnp.int32) for x in arrays] + [
        pltpu.SemaphoreType.DMA((len(arrays),))
    ]


def owner_pairs(block, parity, distance=0):
    bricks, subs, chans = (lax.axis_size(axis) for axis in ("brick", "sub", "chan"))

    def device(owner, chan):
        return (owner // subs * chans + chan % chans) * subs + owner % subs

    pairs = [(o, o + 1) for o in range(parity, bricks * subs - 1, 2)]
    pairs += [(b, a) for a, b in pairs]
    route = [(device(a, c + distance), device(b, c)) for a, b in pairs for c in range(chans)]
    return lax.ppermute(block, ("brick", "chan", "sub"), route)


def from_ahead(block, axis, distance):
    n = lax.axis_size(axis)
    return lax.ppermute(block, axis, [((i + distance) % n, i) for i in range(n)])


def to_ahead(block, axis, distance):
    n = lax.axis_size(axis)
    return lax.ppermute(block, axis, [(i, (i + distance) % n) for i in range(n)])


def sorted_rows(scan_order, features):
    total = features.shape[0]
    taken = scan_order.reshape(total, 1) == jnp.arange(total, dtype=jnp.int32)[None]
    return jnp.dot(taken.astype(BF16), features, preferred_element_type=F32).astype(BF16)


def assemble_kernel(bricks, subs, chans, keys, halo_near, *refs):
    parts, (rows, even, odd, halo, semaphore) = dict(zip(keys, refs[:-5])), refs[-5:]
    reach = halo.shape[1]
    scalars = Scalars([halo_near], [halo], semaphore)
    place = Place()
    split = BLK // parts[0, 0].shape[1]
    for (jb, j), part in parts.items():
        source = lax.rem(place.brick - jb + bricks, bricks)
        chan = lax.rem(place.chan + j, chans)
        for js in range(subs):
            sub = lax.rem(place.sub + js, subs)
            rows[(source * subs + sub) * chans + chan] = part[js]
    scalars.wait()
    for j in range(reach):
        even[pl.ds(j * split, split)] = rows[pl.ds(halo[place.parity, j] * split, split)]
        odd[pl.ds(j * split, split)] = rows[pl.ds(halo[1 - place.parity, j] * split, split)]


def assemble(halo, parts, bricks, subs, chans):
    per, channels = parts[0, 0].shape[1:]
    pieces = bricks * subs * chans
    split = BLK // per
    sent = halo.shape[1] * split
    return pl.pallas_call(
        functools.partial(assemble_kernel, bricks, subs, chans, tuple(parts)),
        out_shape=[
            jax.ShapeDtypeStruct((count, per, channels), BF16) for count in (pieces, sent, sent)
        ],
        in_specs=[VMEM] * (1 + len(parts)),
        out_specs=[VMEM] * 3,
        scratch_shapes=scalar_scratch(halo),
        compiler_params=LIMIT,
        name="assemble",
    )(halo, *parts.values())


def block_sums(table, blocks, weight, total):
    count = table.shape[0]
    group = min(count, 16)
    lanes = blocks.shape[2]
    offsets = weight.shape[2] // lanes

    def one_group(g, carry):
        first = g * group
        running = None
        for w in range(weight.shape[0]):
            inside = range(w * offsets, min((w + 1) * offsets, table.shape[1]))
            picked = jnp.concatenate(
                [
                    jnp.concatenate(
                        [blocks[jnp.minimum(table[first + n, k], count)] for k in inside], axis=1
                    )
                    for n in range(group)
                ],
                axis=0,
            )
            product = lax.dot_general(
                picked, weight[w, :, : len(inside) * lanes], NT, preferred_element_type=F32
            )
            running = product if running is None else running + product
        total[pl.ds(first, group)] = running.reshape(group, BLK, weight.shape[1])
        return carry

    if count == group:
        one_group(0, 0)
    else:
        lax.fori_loop(0, count // group, one_group, 0)


def rim_blocks(place, even, odd, lanes, rim):
    reach = even.shape[0]
    rim[pl.ds(reach * (1 - place.parity), reach), :, lanes] = even[...]
    rim[pl.ds(reach * place.parity, reach), :, lanes] = odd[...]


def named_sums(table, scalars, given, weight, products, total):
    blocks, offsets = given.shape[0], table.shape[1]
    width, channels = weight.shape[1:]
    together = max(1, channels // width)
    rows = given[...].reshape(blocks * BLK, channels)
    for k in range(0, offsets, together):
        size = min(together, offsets - k)
        product = lax.dot_general(
            rows,
            weight[k : k + size].reshape(size * width, channels),
            NT,
            preferred_element_type=F32,
        )
        for i in range(size):
            products[k + i, 0:blocks] = product[:, i * width : (i + 1) * width].reshape(
                blocks, BLK, width
            )
    products[:, blocks : blocks + 1] = jnp.zeros((offsets, 1, BLK, width), F32)
    scalars.wait()

    def one_block(n, carry):
        running = total[n]
        for k in range(offsets):
            running = running + products[k, table[n, k]]
        total[n] = running
        return carry

    lax.fori_loop(0, table.shape[0], one_block, 0, unroll=min(table.shape[0], 16))


def cost(blocks, weight):
    offsets, width, channels = weight.shape
    return pl.CostEstimate(
        flops=4 * blocks * BLK * offsets * width * channels, bytes_accessed=0, transcendentals=0
    )


def own_first_kernel(table_near, rows, weight, total, blocks, table, semaphore):
    scalars = Scalars([table_near], [table], semaphore)
    count = rows.shape[0]
    blocks[0:count] = rows[...]
    blocks[count] = jnp.zeros(blocks.shape[1:], BF16)
    scalars.wait()
    block_sums(table, blocks, weight, total)


def own_first(table, rows, weight):
    count, channels = rows.shape[0], rows.shape[2]
    return pl.pallas_call(
        own_first_kernel,
        out_shape=jax.ShapeDtypeStruct((count, BLK, weight.shape[1]), F32),
        in_specs=[VMEM] * 3,
        out_specs=VMEM,
        scratch_shapes=[pltpu.VMEM((count + 1, BLK, channels), BF16)] + scalar_scratch(table),
        compiler_params=LIMIT,
        cost_estimate=cost(count, weight),
        name="own_first",
    )(table, rows, weight)


def pieces_first_kernel(bricks, subs, behind, started, table_near, weight, *refs):
    parts, (total, held, products, table, semaphore) = refs[:-5], refs[-5:]
    scalars = Scalars([table_near], [table], semaphore)
    if started:
        parts, before = parts[:-1], parts[-1]
    place = Place()
    for jb, part in zip(behind, parts):
        source = lax.rem(place.brick - jb + bricks, bricks)
        for js in range(subs):
            held[source * subs + lax.rem(place.sub + js, subs)] = part[js]
    total[...] = before[...] if started else jnp.zeros(total.shape, F32)
    named_sums(table, scalars, held, weight, products, total)


def pieces_first(table, weight, parts, before, j, bricks, subs):
    offsets, width, channels = weight.shape
    sums = jax.ShapeDtypeStruct((table.shape[0], BLK, width), F32)
    held = bricks * subs
    behind = tuple(jb for jb, far in parts if far == j)
    given = [parts[jb, j] for jb in behind] + ([] if before is None else [before])
    return pl.pallas_call(
        functools.partial(pieces_first_kernel, bricks, subs, behind, before is not None),
        out_shape=sums,
        in_specs=[VMEM] * (2 + len(given)),
        out_specs=VMEM,
        scratch_shapes=[
            pltpu.VMEM((held, BLK, channels), BF16),
            pltpu.VMEM((offsets, held + 1, BLK, width), F32),
        ]
        + scalar_scratch(table),
        compiler_params=LIMIT,
        cost_estimate=cost(held, weight),
        name="pieces_first",
    )(table, weight, *given)


def rim_first_kernel(halo_near, table_near, vectors, own, even, odd, weight, *refs):
    hidden, even_out, odd_out, rim, products, total, halo, table, semaphore = refs
    scalars = Scalars([halo_near, table_near], [halo, table], semaphore)
    reach = even.shape[0]
    place = Place()
    rim_blocks(place, even, odd, slice(None), rim)
    total[...] = own[...]
    named_sums(table, scalars, rim, weight, products, total)
    value = total[...] * vectors[0:1][None] + vectors[1:2][None]
    hidden[...] = jnp.maximum(value, 0.0).astype(BF16)
    for j in range(reach):
        even_out[j] = hidden[halo[place.parity, j]]
        odd_out[j] = hidden[halo[1 - place.parity, j]]


def rim_scratch(count, reach, weight):
    offsets, width, channels = weight.shape
    return [
        pltpu.VMEM((2 * reach, BLK, channels), BF16),
        pltpu.VMEM((offsets, 2 * reach + 1, BLK, width), F32),
        pltpu.VMEM((count, BLK, width), F32),
    ]


def rim_first(halo, table, vectors, own, even, odd, weight):
    count, reach, width = table.shape[0], even.shape[0], weight.shape[1]
    return pl.pallas_call(
        rim_first_kernel,
        out_shape=[
            jax.ShapeDtypeStruct((n, BLK, width), BF16) for n in (count, reach, reach)
        ],
        in_specs=[VMEM] * 7,
        out_specs=[VMEM] * 3,
        scratch_shapes=rim_scratch(count, reach, weight) + scalar_scratch(halo, table),
        compiler_params=LIMIT,
        cost_estimate=cost(2 * reach, weight),
        name="rim_first",
    )(halo, table, vectors, own, even, odd, weight)


def pack_kernel(even, odd, *refs):
    out = refs[-1]
    out[0 : even.shape[0]] = even[...]
    out[even.shape[0] :] = odd[...]


def pack(even, odd, after):
    return pl.pallas_call(
        pack_kernel,
        out_shape=jax.ShapeDtypeStruct((2 * even.shape[0],) + even.shape[1:], BF16),
        in_specs=[VMEM, VMEM] + [pl.BlockSpec(memory_space=pl.ANY)] * len(after),
        out_specs=VMEM,
        compiler_params=LIMIT,
        name="pack",
    )(even, odd, *after)


def own_second_kernel(nearest, chans, table_near, weight, *refs):
    parts, (total, blocks, beside, table, semaphore) = refs[:-5], refs[-5:]
    scalars = Scalars([table_near], [table], semaphore)
    count, width = parts[0].shape[0], parts[0].shape[2]
    place = Place()
    lanes = blocks.shape[2]
    offsets = beside.shape[2] // lanes
    for i, part in enumerate(parts):
        blocks[0:count, :, i * width : (i + 1) * width] = part[...]
        for c in range(chans):

            @pl.when(lax.rem(place.chan + nearest + i, chans) == c)
            def _(i=i, c=c):
                for k in range(weight.shape[0]):
                    at = k % offsets * lanes + i * width
                    beside[k // offsets, :, at : at + width] = weight[
                        k, :, c * width : (c + 1) * width
                    ]

    blocks[count] = jnp.zeros(blocks.shape[1:], BF16)
    scalars.wait()
    block_sums(table, blocks, beside, total)


def own_second(table, weight, parts, nearest, chans):
    count, width = parts[0].shape[0], parts[0].shape[2]
    lanes = width * len(parts)
    offsets = max(1, weight.shape[2] // lanes)
    groups = -(-weight.shape[0] // offsets)
    return pl.pallas_call(
        functools.partial(own_second_kernel, nearest, chans),
        out_shape=jax.ShapeDtypeStruct((count, BLK, width), F32),
        in_specs=[VMEM] * (2 + len(parts)),
        out_specs=VMEM,
        scratch_shapes=[
            pltpu.VMEM((count + 1, BLK, lanes), BF16),
            pltpu.VMEM((groups, width, lanes * offsets), BF16),
        ]
        + scalar_scratch(table),
        compiler_params=LIMIT,
        cost_estimate=cost(count // 2, weight),
        name="own_second",
    )(table, weight, *parts)


def rim_second_kernel(bricks, subs, chans, owns, route_near, table_near, vectors, rows, weight, down_weight, *refs):
    (even, odd), refs = refs[:2], refs[2:]
    sums, refs = refs[:owns], refs[owns:]
    fars, (out, rim, products, total, slots, seen, route, table, semaphore) = refs[:-9], refs[-9:]
    scalars = Scalars([route_near, table_near], [route, table], semaphore)
    count, reach = table.shape[0], even.shape[0]
    width = weight.shape[1]
    place = Place()
    for j in range(chans):
        near = (even, odd) if j == 0 else (fars[j - 1].at[0:reach], fars[j - 1].at[reach:])
        for c in range(chans):

            @pl.when(lax.rem(place.chan + j, chans) == c)
            def _(near=near, c=c):
                rim_blocks(place, *near, slice(c * width, (c + 1) * width), rim)

    total[...] = sums[0][...]
    for more in sums[1:]:
        total[...] += more[...]
    named_sums(table, scalars, rim, weight, products, total)
    for c in range(chans):

        @pl.when(place.chan == c)
        def _(c=c):
            total[...] = (
                total[...] * vectors[2:3][None]
                + vectors[3:4][None]
                + rows[:, :, c * width : (c + 1) * width].astype(F32)
            )

    refined = jnp.maximum(total[...], 0.0).reshape(count, CHILDREN, CELLS, width)
    coarse = None
    for o in range(CHILDREN):
        child = refined[:, o].reshape(count * CELLS, width).astype(BF16)
        product = lax.dot_general(child, down_weight[o], NN, preferred_element_type=F32)
        coarse = product if coarse is None else coarse + product
    slots[...] = jnp.full(slots.shape, ABSENT, F32)
    for owner in range(bricks * subs):
        seen[owner] = 0
    for n in range(count):
        owner = route[0, n]
        slot = seen[owner]
        seen[owner] = slot + 1
        device = owner // subs * (chans * subs) + lax.rem(owner, subs)
        for c in range(chans):
            slots[device + c * subs, pl.ds(pl.multiple_of(slot * CELLS, CELLS), CELLS)] = coarse[
                n * CELLS : (n + 1) * CELLS, c * width : (c + 1) * width
            ]
    out[...] = slots[...].astype(BF16)


def rim_second(route, table, vectors, rows, weight, down_weight, even, odd, sums, fars, bricks, subs, chans, capacity):
    count, reach, width = table.shape[0], even.shape[0], weight.shape[1]
    slots = (bricks * subs * chans, capacity * CELLS, width)
    return pl.pallas_call(
        functools.partial(rim_second_kernel, bricks, subs, chans, len(sums)),
        out_shape=jax.ShapeDtypeStruct(slots, BF16),
        in_specs=[VMEM] * (8 + len(sums) + len(fars)),
        out_specs=VMEM,
        scratch_shapes=rim_scratch(count, reach, weight)
        + [pltpu.VMEM(slots, F32), pltpu.SMEM((bricks * subs,), jnp.int32)]
        + scalar_scratch(route, table),
        compiler_params=LIMIT,
        cost_estimate=cost(2 * reach, weight),
        name="rim_second",
    )(route, table, vectors, rows, weight, down_weight, even, odd, *sums, *fars)


def arrive_kernel(bricks, subs, chans, vectors, parts, out):
    held = []
    for b in range(bricks):
        for s in range(subs):
            coarse = None
            for c in range(chans):
                part = parts[(b * chans + c) * subs + s].astype(F32)
                coarse = part if coarse is None else coarse + part
            held.append(coarse)
    coarse = jnp.concatenate(held, axis=0)
    tiles = jnp.maximum(coarse * vectors[4:5] + vectors[5:6], 0.0)
    tiles = jnp.where(coarse < ABSENT / 2, 0.0, tiles)
    out[0] = tiles.T.astype(BF16)


def arrived_tiles(vectors, parts, bricks, subs, chans):
    slots, width = parts.shape[1:]
    return pl.pallas_call(
        functools.partial(arrive_kernel, bricks, subs, chans),
        out_shape=jax.ShapeDtypeStruct((1, width, bricks * subs * slots), BF16),
        in_specs=[VMEM, VMEM],
        out_specs=VMEM,
        compiler_params=LIMIT,
        name="arrived_tiles",
    )(vectors, parts)


def to_owners(ordered, chans):
    bricks, subs = ordered.shape[:2]
    brick, sub = lax.axis_index("brick"), lax.axis_index("sub")

    def pieces(js):
        column = lax.dynamic_index_in_dim(ordered, lax.rem(sub + js, subs), 1, keepdims=False)
        doubled = jnp.concatenate([column, column], axis=0)
        return lax.dynamic_slice_in_dim(doubled, brick, bricks, 0)

    by_sub = [pieces(0)]
    for js in range(1, subs):
        by_sub.append(to_ahead(pieces(subs - js), "sub", subs - js))
    stacked = [jnp.stack([piece[jb] for piece in by_sub]) for jb in range(bricks)]
    order = sorted(range(1, bricks), key=lambda jb: min(jb, bricks - jb))
    parts = {(0, 0): stacked[0]}
    for jb in order:
        parts[jb, 0] = to_ahead(stacked[jb], "brick", jb)
    for jb in [0] + order:
        for j in range(1, chans):
            parts[jb, j] = from_ahead(parts[jb, 0], "chan", j)
    return parts


def body(
    features,
    scan_order,
    kernel_map,
    halo_send,
    down_route,
    conv1_weight,
    conv2_weight,
    down_weight,
    gain_first,
    bias_first,
    gain_second,
    bias_second,
    gain_down,
    bias_down,
):
    bricks, subs, chans = (lax.axis_size(axis) for axis in ("brick", "sub", "chan"))
    owners = bricks * subs
    count, reach = kernel_map.shape[0], halo_send.shape[1]
    channels = features.shape[1]
    ordered = sorted_rows(scan_order, features)
    ordered = ordered.reshape(bricks, subs, features.shape[0] // owners, channels)
    parts = to_owners(ordered, chans)
    chan = lax.axis_index("chan")
    down_route = down_route.reshape(1, count)
    vectors = jnp.stack(
        [gain_first, bias_first, gain_second, bias_second, gain_down, bias_down]
    )
    rows, even, odd = assemble(halo_send, parts, bricks, subs, chans)
    rows = rows.reshape(count, BLK, channels)
    even = owner_pairs(even, 0).reshape(reach, BLK, channels)
    odd = owner_pairs(odd, 1).reshape(reach, BLK, channels)
    outside = jnp.where(kernel_map < count, 2 * reach, kernel_map - count)
    if features.shape[0] // owners == BLK:
        own = None
        for j in range(chans):
            here = (kernel_map < count) & (lax.rem(kernel_map, chans) == lax.rem(chan + j, chans))
            inside = jnp.where(here, lax.div(kernel_map, chans), owners)
            own = pieces_first(inside, conv1_weight, parts, own, j, bricks, subs)
    else:
        own = own_first(kernel_map, rows, conv1_weight)
    hidden, even, odd = rim_first(halo_send, outside, vectors, own, even, odd, conv1_weight)
    others = [from_ahead(hidden, "chan", j) for j in range(1, chans)]
    even, odd = owner_pairs(even, 0), owner_pairs(odd, 1)
    sums = [own_second(kernel_map, conv2_weight, [hidden], 0, chans)]
    rim = pack(even, odd, sums)
    fars = [from_ahead(rim, "chan", j) for j in range(1, chans)]
    if others:
        sums.append(own_second(kernel_map, conv2_weight, others, 1, chans))
    capacity = max(2, 2 * count // owners)
    partial = rim_second(
        down_route,
        outside,
        vectors,
        rows,
        conv2_weight,
        down_weight,
        even,
        odd,
        sums,
        fars,
        bricks,
        subs,
        chans,
        capacity,
    )
    partial = lax.all_to_all(
        partial, ("brick", "chan", "sub"), split_axis=0, concat_axis=0, tiled=True
    )
    return arrived_tiles(vectors, partial, bricks, subs, chans)


def solution(mesh):
    placed = (
        P(("groups", "brick", "chan", "sub"), None),
        P(("groups", "brick", "chan", "sub"), None),
        P(("groups", "brick", "sub"), None),
        P(("groups", "brick", "sub"), None),
        P(("groups", "brick", "sub"), None),
        P(None, "chan", None),
        P(None, "chan", None),
        P(None, "chan", None),
        P("chan"),
        P("chan"),
        P("chan"),
        P("chan"),
        P("chan"),
        P("chan"),
    )
    return jax.shard_map(
        body,
        mesh=mesh,
        in_specs=placed,
        out_specs=P(("groups", "brick", "sub"), "chan", None),
        check_vma=False,
    )
```

```python
import functools

import jax
import jax.numpy as jnp
from jax import lax
from jax.experimental import pallas as pl
from jax.experimental.pallas import tpu as pltpu
from jax.sharding import PartitionSpec as P

BLK = 64
CHILDREN = 8
CELLS = BLK // CHILDREN
ABSENT = -1e30
F32 = jnp.float32
BF16 = jnp.bfloat16
NT = (((1,), (1,)), ((), ()))
NN = (((1,), (0,)), ((), ()))
VMEM = pl.BlockSpec(memory_space=pltpu.VMEM)
LIMIT = pltpu.CompilerParams(vmem_limit_bytes=40 * 2**20)


class Place:
    def __init__(self):
        self.brick, self.sub, self.chan = (lax.axis_index(a) for a in ("brick", "sub", "chan"))
        self.parity = lax.rem(self.brick * lax.axis_size("sub") + self.sub, 2)


class Scalars:
    def __init__(self, given, held, semaphore):
        self.copies = [
            pltpu.make_async_copy(source, target, semaphore.at[i])
            for i, (source, target) in enumerate(zip(given, held))
        ]
        for copy in self.copies:
            copy.start()

    def wait(self):
        for copy in self.copies:
            copy.wait()


def scalar_scratch(*arrays):
    return [pltpu.SMEM(x.shape, jnp.int32) for x in arrays] + [
        pltpu.SemaphoreType.DMA((len(arrays),))
    ]


def owner_pairs(block, parity):
    owners = lax.axis_size("brick") * lax.axis_size("sub")
    pairs = [(o, o + 1) for o in range(parity, owners - 1, 2)]
    if parity == 1 and owners % 2 == 0:
        pairs.append((0, owners - 1))
    return lax.ppermute(block, ("brick", "sub"), pairs + [(b, a) for a, b in pairs])


def named(place, odd):
    owners = lax.axis_size("brick") * lax.axis_size("sub")
    owner = place.brick * lax.axis_size("sub") + place.sub
    inside = (owner > 0) & ((owner < owners - 1) | (place.parity == 0))
    return jnp.where(inside, odd, jnp.zeros_like(odd))


def from_ahead(block, axis, distance):
    n = lax.axis_size(axis)
    return lax.ppermute(block, axis, [((i + distance) % n, i) for i in range(n)])


def other(brick, step, bricks, way=1):
    if bricks & (bricks - 1) == 0:
        return brick ^ step
    return (brick + way * step + bricks) % bricks


def across(block, step):
    bricks = lax.axis_size("brick")
    return lax.ppermute(block, "brick", [(b, other(b, step, bricks)) for b in range(bricks)])


def to_ahead(block, axis, distance):
    n = lax.axis_size(axis)
    return lax.ppermute(block, axis, [(i, (i + distance) % n) for i in range(n)])


def sorted_rows(scan_order, features):
    total = features.shape[0]
    taken = scan_order.reshape(total, 1) == jnp.arange(total, dtype=jnp.int32)[None]
    return jnp.dot(taken.astype(BF16), features, preferred_element_type=F32).astype(BF16)


def assemble_kernel(bricks, subs, chans, keys, halo_near, *refs):
    parts, (rows, even, odd, halo, semaphore) = dict(zip(keys, refs[:-5])), refs[-5:]
    reach = halo.shape[1]
    scalars = Scalars([halo_near], [halo], semaphore)
    place = Place()
    split = BLK // parts[0, 0].shape[1]
    for (jb, j), part in parts.items():
        source = other(place.brick, jb, bricks, -1)
        chan = lax.rem(place.chan + j, chans)
        for js in range(subs):
            sub = lax.rem(place.sub + js, subs)
            rows[(source * subs + sub) * chans + chan] = part[js]
    scalars.wait()
    for j in range(reach):
        even[pl.ds(j * split, split)] = rows[pl.ds(halo[place.parity, j] * split, split)]
        odd[pl.ds(j * split, split)] = rows[pl.ds(halo[1 - place.parity, j] * split, split)]


def assemble(halo, parts, bricks, subs, chans):
    per, channels = parts[0, 0].shape[1:]
    pieces = bricks * subs * chans
    split = BLK // per
    sent = halo.shape[1] * split
    return pl.pallas_call(
        functools.partial(assemble_kernel, bricks, subs, chans, tuple(parts)),
        out_shape=[
            jax.ShapeDtypeStruct((count, per, channels), BF16) for count in (pieces, sent, sent)
        ],
        in_specs=[VMEM] * (1 + len(parts)),
        out_specs=[VMEM] * 3,
        scratch_shapes=scalar_scratch(halo),
        compiler_params=LIMIT,
        name="assemble",
    )(halo, *parts.values())


def block_sums(table, blocks, weight, total):
    count = table.shape[0]
    group = min(count, 16)
    lanes = blocks.shape[2]
    offsets = weight.shape[2] // lanes

    def one_group(g, carry):
        first = g * group
        running = None
        for w in range(weight.shape[0]):
            inside = range(w * offsets, min((w + 1) * offsets, table.shape[1]))
            picked = jnp.concatenate(
                [
                    jnp.concatenate(
                        [blocks[jnp.minimum(table[first + n, k], count)] for k in inside], axis=1
                    )
                    for n in range(group)
                ],
                axis=0,
            )
            product = lax.dot_general(
                picked, weight[w, :, : len(inside) * lanes], NT, preferred_element_type=F32
            )
            running = product if running is None else running + product
        total[pl.ds(first, group)] = running.reshape(group, BLK, weight.shape[1])
        return carry

    if count == group:
        one_group(0, 0)
    else:
        lax.fori_loop(0, count // group, one_group, 0)


def rim_blocks(place, even, odd, lanes, rim):
    reach = even.shape[0]
    rim[pl.ds(reach * (1 - place.parity), reach), :, lanes] = even[...]
    rim[pl.ds(reach * place.parity, reach), :, lanes] = named(place, odd[...])


def named_sums(table, scalars, given, weight, products, total):
    blocks, offsets = given.shape[0], table.shape[1]
    width, channels = weight.shape[1:]
    together = max(1, channels // width)
    rows = given[...].reshape(blocks * BLK, channels)
    for k in range(0, offsets, together):
        size = min(together, offsets - k)
        product = lax.dot_general(
            rows,
            weight[k : k + size].reshape(size * width, channels),
            NT,
            preferred_element_type=F32,
        )
        for i in range(size):
            products[k + i, 0:blocks] = product[:, i * width : (i + 1) * width].reshape(
                blocks, BLK, width
            )
    products[:, blocks : blocks + 1] = jnp.zeros((offsets, 1, BLK, width), F32)
    scalars.wait()

    def one_block(n, carry):
        running = total[n]
        for k in range(offsets):
            running = running + products[k, table[n, k]]
        total[n] = running
        return carry

    lax.fori_loop(0, table.shape[0], one_block, 0, unroll=min(table.shape[0], 16))


def cost(blocks, weight):
    offsets, width, channels = weight.shape
    return pl.CostEstimate(
        flops=4 * blocks * BLK * offsets * width * channels, bytes_accessed=0, transcendentals=0
    )


def own_first_kernel(table_near, rows, weight, total, blocks, table, semaphore):
    scalars = Scalars([table_near], [table], semaphore)
    count = rows.shape[0]
    blocks[0:count] = rows[...]
    blocks[count] = jnp.zeros(blocks.shape[1:], BF16)
    scalars.wait()
    block_sums(table, blocks, weight, total)


def own_first(table, rows, weight):
    count, channels = rows.shape[0], rows.shape[2]
    return pl.pallas_call(
        own_first_kernel,
        out_shape=jax.ShapeDtypeStruct((count, BLK, weight.shape[1]), F32),
        in_specs=[VMEM] * 3,
        out_specs=VMEM,
        scratch_shapes=[pltpu.VMEM((count + 1, BLK, channels), BF16)] + scalar_scratch(table),
        compiler_params=LIMIT,
        cost_estimate=cost(count, weight),
        name="own_first",
    )(table, rows, weight)


def pieces_first_kernel(bricks, subs, behind, started, table_near, weight, *refs):
    parts, (total, held, products, table, semaphore) = refs[:-5], refs[-5:]
    scalars = Scalars([table_near], [table], semaphore)
    if started:
        parts, before = parts[:-1], parts[-1]
    place = Place()
    for jb, part in zip(behind, parts):
        source = other(place.brick, jb, bricks, -1)
        for js in range(subs):
            held[source * subs + lax.rem(place.sub + js, subs)] = part[js]
    total[...] = before[...] if started else jnp.zeros(total.shape, F32)
    named_sums(table, scalars, held, weight, products, total)


def pieces_first(table, weight, parts, before, j, bricks, subs):
    offsets, width, channels = weight.shape
    sums = jax.ShapeDtypeStruct((table.shape[0], BLK, width), F32)
    held = bricks * subs
    behind = tuple(jb for jb, far in parts if far == j)
    given = [parts[jb, j] for jb in behind] + ([] if before is None else [before])
    return pl.pallas_call(
        functools.partial(pieces_first_kernel, bricks, subs, behind, before is not None),
        out_shape=sums,
        in_specs=[VMEM] * (2 + len(given)),
        out_specs=VMEM,
        scratch_shapes=[
            pltpu.VMEM((held, BLK, channels), BF16),
            pltpu.VMEM((offsets, held + 1, BLK, width), F32),
        ]
        + scalar_scratch(table),
        compiler_params=LIMIT,
        cost_estimate=cost(held, weight),
        name="pieces_first",
    )(table, weight, *given)


def rim_first_kernel(odd, even, halo_near, table_near, vectors, own, weight, *refs):
    hidden, even_out, odd_out, rim, products, total, halo, table, semaphore = refs
    scalars = Scalars([halo_near, table_near], [halo, table], semaphore)
    reach = even.shape[0]
    place = Place()
    rim_blocks(place, even, odd, slice(None), rim)
    total[...] = own[...]
    named_sums(table, scalars, rim, weight, products, total)
    value = total[...] * vectors[0:1][None] + vectors[1:2][None]
    hidden[...] = jnp.maximum(value, 0.0).astype(BF16)
    for j in range(reach):
        even_out[j] = hidden[halo[place.parity, j]]
        odd_out[j] = hidden[halo[1 - place.parity, j]]


def rim_scratch(count, reach, weight):
    offsets, width, channels = weight.shape
    return [
        pltpu.VMEM((2 * reach, BLK, channels), BF16),
        pltpu.VMEM((offsets, 2 * reach + 1, BLK, width), F32),
        pltpu.VMEM((count, BLK, width), F32),
    ]


def rim_first(halo, table, vectors, own, even, odd, weight):
    count, reach, width = table.shape[0], even.shape[0], weight.shape[1]
    return pl.pallas_call(
        rim_first_kernel,
        out_shape=[
            jax.ShapeDtypeStruct((n, BLK, width), BF16) for n in (count, reach, reach)
        ],
        in_specs=[VMEM] * 7,
        out_specs=[VMEM] * 3,
        scratch_shapes=rim_scratch(count, reach, weight) + scalar_scratch(halo, table),
        compiler_params=LIMIT,
        cost_estimate=cost(2 * reach, weight),
        name="rim_first",
    )(odd, even, halo, table, vectors, own, weight)


def pack_kernel(even, odd, *refs):
    out = refs[-1]
    out[0 : even.shape[0]] = even[...]
    out[even.shape[0] :] = odd[...]


def pack(even, odd, after):
    return pl.pallas_call(
        pack_kernel,
        out_shape=jax.ShapeDtypeStruct((2 * even.shape[0],) + even.shape[1:], BF16),
        in_specs=[VMEM, VMEM] + [pl.BlockSpec(memory_space=pl.ANY)] * len(after),
        out_specs=VMEM,
        compiler_params=LIMIT,
        name="pack",
    )(even, odd, *after)


def own_second_kernel(nearest, chans, table_near, weight, *refs):
    parts, (total, blocks, beside, table, semaphore) = refs[:-5], refs[-5:]
    scalars = Scalars([table_near], [table], semaphore)
    count, width = parts[0].shape[0], parts[0].shape[2]
    place = Place()
    lanes = blocks.shape[2]
    offsets = beside.shape[2] // lanes
    for i, part in enumerate(parts):
        blocks[0:count, :, i * width : (i + 1) * width] = part[...]
        for c in range(chans):

            @pl.when(lax.rem(place.chan + nearest + i, chans) == c)
            def _(i=i, c=c):
                for k in range(weight.shape[0]):
                    at = k % offsets * lanes + i * width
                    beside[k // offsets, :, at : at + width] = weight[
                        k, :, c * width : (c + 1) * width
                    ]

    blocks[count] = jnp.zeros(blocks.shape[1:], BF16)
    scalars.wait()
    block_sums(table, blocks, beside, total)


def own_second(table, weight, parts, nearest, chans):
    count, width = parts[0].shape[0], parts[0].shape[2]
    lanes = width * len(parts)
    offsets = max(1, weight.shape[2] // lanes)
    groups = -(-weight.shape[0] // offsets)
    return pl.pallas_call(
        functools.partial(own_second_kernel, nearest, chans),
        out_shape=jax.ShapeDtypeStruct((count, BLK, width), F32),
        in_specs=[VMEM] * (2 + len(parts)),
        out_specs=VMEM,
        scratch_shapes=[
            pltpu.VMEM((count + 1, BLK, lanes), BF16),
            pltpu.VMEM((groups, width, lanes * offsets), BF16),
        ]
        + scalar_scratch(table),
        compiler_params=LIMIT,
        cost_estimate=cost(count // 2, weight),
        name="own_second",
    )(table, weight, *parts)


def rim_second_kernel(bricks, subs, chans, owns, route_near, table_near, vectors, rows, weight, down_weight, *refs):
    (even, odd), refs = refs[:2], refs[2:]
    sums, refs = refs[:owns], refs[owns:]
    fars, (out, rim, products, total, slots, seen, route, table, semaphore) = refs[:-9], refs[-9:]
    scalars = Scalars([route_near, table_near], [route, table], semaphore)
    count, reach = table.shape[0], even.shape[0]
    width = weight.shape[1]
    place = Place()
    for j in range(chans):
        near = (even, odd) if j == 0 else (fars[j - 1].at[0:reach], fars[j - 1].at[reach:])
        for c in range(chans):

            @pl.when(lax.rem(place.chan + j, chans) == c)
            def _(near=near, c=c):
                rim_blocks(place, *near, slice(c * width, (c + 1) * width), rim)

    total[...] = sums[0][...]
    for more in sums[1:]:
        total[...] += more[...]
    named_sums(table, scalars, rim, weight, products, total)
    for c in range(chans):

        @pl.when(place.chan == c)
        def _(c=c):
            total[...] = (
                total[...] * vectors[2:3][None]
                + vectors[3:4][None]
                + rows[:, :, c * width : (c + 1) * width].astype(F32)
            )

    refined = jnp.maximum(total[...], 0.0).reshape(count, CHILDREN, CELLS, width)
    coarse = None
    for o in range(CHILDREN):
        child = refined[:, o].reshape(count * CELLS, width).astype(BF16)
        product = lax.dot_general(child, down_weight[o], NN, preferred_element_type=F32)
        coarse = product if coarse is None else coarse + product
    slots[...] = jnp.full(slots.shape, ABSENT, F32)
    for owner in range(bricks * subs):
        seen[owner] = 0
    for n in range(count):
        owner = route[0, n]
        slot = seen[owner]
        seen[owner] = slot + 1
        device = owner // subs * (chans * subs) + lax.rem(owner, subs)
        for c in range(chans):
            slots[device + c * subs, pl.ds(pl.multiple_of(slot * CELLS, CELLS), CELLS)] = coarse[
                n * CELLS : (n + 1) * CELLS, c * width : (c + 1) * width
            ]
    out[...] = slots[...].astype(BF16)


def rim_second(route, table, vectors, rows, weight, down_weight, even, odd, sums, fars, bricks, subs, chans, capacity):
    count, reach, width = table.shape[0], even.shape[0], weight.shape[1]
    slots = (bricks * subs * chans, capacity * CELLS, width)
    return pl.pallas_call(
        functools.partial(rim_second_kernel, bricks, subs, chans, len(sums)),
        out_shape=jax.ShapeDtypeStruct(slots, BF16),
        in_specs=[VMEM] * (8 + len(sums) + len(fars)),
        out_specs=VMEM,
        scratch_shapes=rim_scratch(count, reach, weight)
        + [pltpu.VMEM(slots, F32), pltpu.SMEM((bricks * subs,), jnp.int32)]
        + scalar_scratch(route, table),
        compiler_params=LIMIT,
        cost_estimate=cost(2 * reach, weight),
        name="rim_second",
    )(route, table, vectors, rows, weight, down_weight, even, odd, *sums, *fars)


def arrive_kernel(bricks, subs, chans, vectors, parts, out):
    held = []
    for b in range(bricks):
        for s in range(subs):
            coarse = None
            for c in range(chans):
                part = parts[(b * chans + c) * subs + s].astype(F32)
                coarse = part if coarse is None else coarse + part
            held.append(coarse)
    coarse = jnp.concatenate(held, axis=0)
    tiles = jnp.maximum(coarse * vectors[4:5] + vectors[5:6], 0.0)
    tiles = jnp.where(coarse < ABSENT / 2, 0.0, tiles)
    out[0] = tiles.T.astype(BF16)


def arrived_tiles(vectors, parts, bricks, subs, chans):
    slots, width = parts.shape[1:]
    return pl.pallas_call(
        functools.partial(arrive_kernel, bricks, subs, chans),
        out_shape=jax.ShapeDtypeStruct((1, width, bricks * subs * slots), BF16),
        in_specs=[VMEM, VMEM],
        out_specs=VMEM,
        compiler_params=LIMIT,
        name="arrived_tiles",
    )(vectors, parts)


def to_owners(ordered, chans):
    bricks, subs = ordered.shape[:2]
    brick, sub = lax.axis_index("brick"), lax.axis_index("sub")

    def pieces(js):
        column = lax.dynamic_index_in_dim(ordered, lax.rem(sub + js, subs), 1, keepdims=False)
        return jnp.stack(
            [
                lax.dynamic_index_in_dim(column, other(brick, jb, bricks), 0, keepdims=False)
                for jb in range(bricks)
            ]
        )

    by_sub = [pieces(0)]
    for js in range(1, subs):
        by_sub.append(to_ahead(pieces(subs - js), "sub", subs - js))
    stacked = [jnp.stack([piece[jb] for piece in by_sub]) for jb in range(bricks)]
    order = sorted(range(1, bricks), key=lambda jb: (jb % 2 == 0, -jb))
    parts = {(0, 0): stacked[0]}
    for jb in order:
        parts[jb, 0] = across(stacked[jb], jb)
    for jb in [0] + order:
        for j in range(1, chans):
            parts[jb, j] = from_ahead(parts[jb, 0], "chan", j)
    return parts


def body(
    features,
    scan_order,
    kernel_map,
    halo_send,
    down_route,
    conv1_weight,
    conv2_weight,
    down_weight,
    gain_first,
    bias_first,
    gain_second,
    bias_second,
    gain_down,
    bias_down,
):
    bricks, subs, chans = (lax.axis_size(axis) for axis in ("brick", "sub", "chan"))
    owners = bricks * subs
    count, reach = kernel_map.shape[0], halo_send.shape[1]
    channels = features.shape[1]
    ordered = sorted_rows(scan_order, features)
    ordered = ordered.reshape(bricks, subs, features.shape[0] // owners, channels)
    parts = to_owners(ordered, chans)
    chan = lax.axis_index("chan")
    down_route = down_route.reshape(1, count)
    vectors = jnp.stack(
        [gain_first, bias_first, gain_second, bias_second, gain_down, bias_down]
    )
    rows, even, odd = assemble(halo_send, parts, bricks, subs, chans)
    rows = rows.reshape(count, BLK, channels)
    even = owner_pairs(even, 0).reshape(reach, BLK, channels)
    odd = owner_pairs(odd, 1).reshape(reach, BLK, channels)
    outside = jnp.where(kernel_map < count, 2 * reach, kernel_map - count)
    if features.shape[0] // owners == BLK:
        own = None
        for j in range(chans):
            here = (kernel_map < count) & (lax.rem(kernel_map, chans) == lax.rem(chan + j, chans))
            inside = jnp.where(here, lax.div(kernel_map, chans), owners)
            own = pieces_first(inside, conv1_weight, parts, own, j, bricks, subs)
    else:
        own = own_first(kernel_map, rows, conv1_weight)
    hidden, even, odd = rim_first(halo_send, outside, vectors, own, even, odd, conv1_weight)
    others = [from_ahead(hidden, "chan", j) for j in range(1, chans)]
    even, odd = owner_pairs(even, 0), owner_pairs(odd, 1)
    sums = [own_second(kernel_map, conv2_weight, [hidden], 0, chans)]
    rim = pack(even, odd, sums)
    fars = [from_ahead(rim, "chan", j) for j in range(1, chans)]
    if others:
        sums.append(own_second(kernel_map, conv2_weight, others, 1, chans))
    capacity = max(2, 2 * count // owners)
    partial = rim_second(
        down_route,
        outside,
        vectors,
        rows,
        conv2_weight,
        down_weight,
        even,
        odd,
        sums,
        fars,
        bricks,
        subs,
        chans,
        capacity,
    )
    partial = lax.all_to_all(
        partial, ("brick", "chan", "sub"), split_axis=0, concat_axis=0, tiled=True
    )
    return arrived_tiles(vectors, partial, bricks, subs, chans)


def solution(mesh):
    placed = (
        P(("groups", "brick", "chan", "sub"), None),
        P(("groups", "brick", "chan", "sub"), None),
        P(("groups", "brick", "sub"), None),
        P(("groups", "brick", "sub"), None),
        P(("groups", "brick", "sub"), None),
        P(None, "chan", None),
        P(None, "chan", None),
        P(None, "chan", None),
        P("chan"),
        P("chan"),
        P("chan"),
        P("chan"),
        P("chan"),
        P("chan"),
    )
    return jax.shard_map(
        body,
        mesh=mesh,
        in_specs=placed,
        out_specs=P(("groups", "brick", "sub"), "chan", None),
        check_vma=False,
    )
```

```python
import functools

import jax
import jax.numpy as jnp
from jax import lax
from jax.experimental import pallas as pl
from jax.experimental.pallas import tpu as pltpu
from jax.sharding import PartitionSpec as P

BLK = 64
CHILDREN = 8
CELLS = BLK // CHILDREN
ABSENT = -1e30
F32 = jnp.float32
BF16 = jnp.bfloat16
NT = (((1,), (1,)), ((), ()))
NN = (((1,), (0,)), ((), ()))
VMEM = pl.BlockSpec(memory_space=pltpu.VMEM)
LIMIT = pltpu.CompilerParams(vmem_limit_bytes=40 * 2**20)


class Place:
    def __init__(self):
        self.brick, self.sub, self.chan = (lax.axis_index(a) for a in ("brick", "sub", "chan"))
        self.parity = lax.rem(self.brick * lax.axis_size("sub") + self.sub, 2)


class Scalars:
    def __init__(self, given, held, semaphore):
        self.copies = [
            pltpu.make_async_copy(source, target, semaphore.at[i])
            for i, (source, target) in enumerate(zip(given, held))
        ]
        for copy in self.copies:
            copy.start()

    def wait(self):
        for copy in self.copies:
            copy.wait()


def scalar_scratch(*arrays):
    return [pltpu.SMEM(x.shape, jnp.int32) for x in arrays] + [
        pltpu.SemaphoreType.DMA((len(arrays),))
    ]


def owner_pairs(block, parity):
    owners = lax.axis_size("brick") * lax.axis_size("sub")
    pairs = [(o, o + 1) for o in range(parity, owners - 1, 2)]
    if parity == 1 and owners % 2 == 0:
        pairs.append((0, owners - 1))
    return lax.ppermute(block, ("brick", "sub"), pairs + [(b, a) for a, b in pairs])


def named(place, odd):
    owners = lax.axis_size("brick") * lax.axis_size("sub")
    owner = place.brick * lax.axis_size("sub") + place.sub
    inside = (owner > 0) & ((owner < owners - 1) | (place.parity == 0))
    return jnp.where(inside, odd, jnp.zeros_like(odd))


def from_ahead(block, axis, distance):
    n = lax.axis_size(axis)
    return lax.ppermute(block, axis, [((i + distance) % n, i) for i in range(n)])


def other(brick, step, bricks, way=1):
    if bricks & (bricks - 1) == 0:
        return brick ^ step
    return (brick + way * step + bricks) % bricks


def across(block, step):
    bricks = lax.axis_size("brick")
    return lax.ppermute(block, "brick", [(b, other(b, step, bricks)) for b in range(bricks)])


def to_ahead(block, axis, distance):
    n = lax.axis_size(axis)
    return lax.ppermute(block, axis, [(i, (i + distance) % n) for i in range(n)])


def sorted_rows(scan_order, features):
    total = features.shape[0]
    taken = scan_order.reshape(total, 1) == jnp.arange(total, dtype=jnp.int32)[None]
    return jnp.dot(taken.astype(BF16), features, preferred_element_type=F32).astype(BF16)


def assemble_kernel(bricks, subs, chans, keys, halo_near, *refs):
    parts, (rows, even, odd) = dict(zip(keys, refs[:-3])), refs[-3:]
    lists, reach = halo_near[...], halo_near.shape[1]
    place = Place()
    split = BLK // parts[0, 0].shape[1]
    for (jb, j), part in parts.items():
        source = other(place.brick, jb, bricks, -1)
        chan = lax.rem(place.chan + j, chans)
        for js in range(subs):
            sub = lax.rem(place.sub + js, subs)
            rows[(source * subs + sub) * chans + chan] = part[js]
    for j in range(reach):
        up, down = lists[0, j], lists[1, j]
        first = jnp.where(place.parity == 0, up, down)
        second = jnp.where(place.parity == 0, down, up)
        even[pl.ds(j * split, split)] = rows[pl.ds(first * split, split)]
        odd[pl.ds(j * split, split)] = rows[pl.ds(second * split, split)]


def assemble(halo, parts, bricks, subs, chans):
    per, channels = parts[0, 0].shape[1:]
    pieces = bricks * subs * chans
    split = BLK // per
    sent = halo.shape[1] * split
    return pl.pallas_call(
        functools.partial(assemble_kernel, bricks, subs, chans, tuple(parts)),
        out_shape=[
            jax.ShapeDtypeStruct((count, per, channels), BF16) for count in (pieces, sent, sent)
        ],
        in_specs=[VMEM] * (1 + len(parts)),
        out_specs=[VMEM] * 3,
        compiler_params=LIMIT,
        name="assemble",
    )(halo, *parts.values())


def block_sums(table, blocks, weight, total):
    count = table.shape[0]
    group = min(count, 16)
    lanes = blocks.shape[2]
    offsets = weight.shape[2] // lanes

    def one_group(g, carry):
        first = g * group
        running = None
        for w in range(weight.shape[0]):
            inside = range(w * offsets, min((w + 1) * offsets, table.shape[1]))
            picked = jnp.concatenate(
                [
                    jnp.concatenate(
                        [blocks[jnp.minimum(table[first + n, k], count)] for k in inside], axis=1
                    )
                    for n in range(group)
                ],
                axis=0,
            )
            product = lax.dot_general(
                picked, weight[w, :, : len(inside) * lanes], NT, preferred_element_type=F32
            )
            running = product if running is None else running + product
        total[pl.ds(first, group)] = running.reshape(group, BLK, weight.shape[1])
        return carry

    if count == group:
        one_group(0, 0)
    else:
        lax.fori_loop(0, count // group, one_group, 0)


def rim_blocks(place, even, odd, lanes, rim):
    reach = even.shape[0]
    rim[pl.ds(reach * (1 - place.parity), reach), :, lanes] = even[...]
    rim[pl.ds(reach * place.parity, reach), :, lanes] = named(place, odd[...])


def named_sums(table, scalars, given, weight, products, begin, end):
    blocks, offsets = given.shape[0], table.shape[1]
    width, channels = weight.shape[1:]
    together = max(1, channels // width)
    rows = given[...].reshape(blocks * BLK, channels)
    for k in range(0, offsets, together):
        size = min(together, offsets - k)
        product = lax.dot_general(
            rows,
            weight[k : k + size].reshape(size * width, channels),
            NT,
            preferred_element_type=F32,
        )
        for i in range(size):
            products[k + i, 0:blocks] = product[:, i * width : (i + 1) * width].reshape(
                blocks, BLK, width
            )
    products[:, blocks : blocks + 1] = jnp.zeros((offsets, 1, BLK, width), F32)
    scalars.wait()

    def one_block(n, carry):
        running = begin(n)
        for k in range(offsets):
            running = running + products[k, table[n, k]]
        end(n, running)
        return carry

    lax.fori_loop(0, table.shape[0], one_block, 0, unroll=min(table.shape[0], 16))


def cost(blocks, weight):
    offsets, width, channels = weight.shape
    return pl.CostEstimate(
        flops=4 * blocks * BLK * offsets * width * channels, bytes_accessed=0, transcendentals=0
    )


def own_first_kernel(table_near, rows, weight, total, blocks, table, semaphore):
    scalars = Scalars([table_near], [table], semaphore)
    count = rows.shape[0]
    blocks[0:count] = rows[...]
    blocks[count] = jnp.zeros(blocks.shape[1:], BF16)
    scalars.wait()
    block_sums(table, blocks, weight, total)


def own_first(table, rows, weight):
    count, channels = rows.shape[0], rows.shape[2]
    return pl.pallas_call(
        own_first_kernel,
        out_shape=jax.ShapeDtypeStruct((count, BLK, weight.shape[1]), F32),
        in_specs=[VMEM] * 3,
        out_specs=VMEM,
        scratch_shapes=[pltpu.VMEM((count + 1, BLK, channels), BF16)] + scalar_scratch(table),
        compiler_params=LIMIT,
        cost_estimate=cost(count, weight),
        name="own_first",
    )(table, rows, weight)


def pieces_first_kernel(bricks, subs, behind, started, table_near, weight, *refs):
    parts, (total, held, products, table, semaphore) = refs[:-5], refs[-5:]
    scalars = Scalars([table_near], [table], semaphore)
    if started:
        parts, before = parts[:-1], parts[-1]
    place = Place()
    for jb, part in zip(behind, parts):
        source = other(place.brick, jb, bricks, -1)
        for js in range(subs):
            held[source * subs + lax.rem(place.sub + js, subs)] = part[js]

    def begin(n):
        return before[n] if started else jnp.zeros(total.shape[1:], F32)

    def end(n, value):
        total[n] = value

    named_sums(table, scalars, held, weight, products, begin, end)


def pieces_first(table, weight, parts, before, j, bricks, subs):
    offsets, width, channels = weight.shape
    sums = jax.ShapeDtypeStruct((table.shape[0], BLK, width), F32)
    held = bricks * subs
    behind = tuple(jb for jb, far in parts if far == j)
    given = [parts[jb, j] for jb in behind] + ([] if before is None else [before])
    return pl.pallas_call(
        functools.partial(pieces_first_kernel, bricks, subs, behind, before is not None),
        out_shape=sums,
        in_specs=[VMEM] * (2 + len(given)),
        out_specs=VMEM,
        scratch_shapes=[
            pltpu.VMEM((held, BLK, channels), BF16),
            pltpu.VMEM((offsets, held + 1, BLK, width), F32),
        ]
        + scalar_scratch(table),
        compiler_params=LIMIT,
        cost_estimate=cost(held, weight),
        name="pieces_first",
    )(table, weight, *given)


def rim_first_kernel(odd, even, halo_near, table_near, vectors, own, weight, *refs):
    hidden, even_out, odd_out, rim, products, halo, table, semaphore = refs
    scalars = Scalars([halo_near, table_near], [halo, table], semaphore)
    reach = even.shape[0]
    place = Place()
    rim_blocks(place, even, odd, slice(None), rim)
    gain, bias = vectors[0:1], vectors[1:2]

    def end(n, value):
        hidden[n] = jnp.maximum(value * gain + bias, 0.0).astype(BF16)

    named_sums(table, scalars, rim, weight, products, lambda n: own[n], end)
    for j in range(reach):
        even_out[j] = hidden[halo[place.parity, j]]
        odd_out[j] = hidden[halo[1 - place.parity, j]]


def rim_scratch(reach, weight):
    offsets, width, channels = weight.shape
    return [
        pltpu.VMEM((2 * reach, BLK, channels), BF16),
        pltpu.VMEM((offsets, 2 * reach + 1, BLK, width), F32),
    ]


def rim_first(halo, table, vectors, own, even, odd, weight):
    count, reach, width = table.shape[0], even.shape[0], weight.shape[1]
    return pl.pallas_call(
        rim_first_kernel,
        out_shape=[
            jax.ShapeDtypeStruct((n, BLK, width), BF16) for n in (count, reach, reach)
        ],
        in_specs=[VMEM] * 7,
        out_specs=[VMEM] * 3,
        scratch_shapes=rim_scratch(reach, weight) + scalar_scratch(halo, table),
        compiler_params=LIMIT,
        cost_estimate=cost(2 * reach, weight),
        name="rim_first",
    )(odd, even, halo, table, vectors, own, weight)


def pack_kernel(even, odd, *refs):
    out = refs[-1]
    out[0 : even.shape[0]] = even[...]
    out[even.shape[0] :] = odd[...]


def pack(even, odd, after):
    return pl.pallas_call(
        pack_kernel,
        out_shape=jax.ShapeDtypeStruct((2 * even.shape[0],) + even.shape[1:], BF16),
        in_specs=[VMEM, VMEM] + [pl.BlockSpec(memory_space=pl.ANY)] * len(after),
        out_specs=VMEM,
        compiler_params=LIMIT,
        name="pack",
    )(even, odd, *after)


def own_second_kernel(nearest, chans, table_near, weight, *refs):
    parts, (total, blocks, beside, table, semaphore) = refs[:-5], refs[-5:]
    scalars = Scalars([table_near], [table], semaphore)
    count, width = parts[0].shape[0], parts[0].shape[2]
    place = Place()
    lanes = blocks.shape[2]
    offsets = beside.shape[2] // lanes
    for i, part in enumerate(parts):
        blocks[0:count, :, i * width : (i + 1) * width] = part[...]
        for c in range(chans):

            @pl.when(lax.rem(place.chan + nearest + i, chans) == c)
            def _(i=i, c=c):
                for k in range(weight.shape[0]):
                    at = k % offsets * lanes + i * width
                    beside[k // offsets, :, at : at + width] = weight[
                        k, :, c * width : (c + 1) * width
                    ]

    blocks[count] = jnp.zeros(blocks.shape[1:], BF16)
    scalars.wait()
    block_sums(table, blocks, beside, total)


def own_second(table, weight, parts, nearest, chans):
    count, width = parts[0].shape[0], parts[0].shape[2]
    lanes = width * len(parts)
    offsets = max(1, weight.shape[2] // lanes)
    groups = -(-weight.shape[0] // offsets)
    return pl.pallas_call(
        functools.partial(own_second_kernel, nearest, chans),
        out_shape=jax.ShapeDtypeStruct((count, BLK, width), F32),
        in_specs=[VMEM] * (2 + len(parts)),
        out_specs=VMEM,
        scratch_shapes=[
            pltpu.VMEM((count + 1, BLK, lanes), BF16),
            pltpu.VMEM((groups, width, lanes * offsets), BF16),
        ]
        + scalar_scratch(table),
        compiler_params=LIMIT,
        cost_estimate=cost(count // 2, weight),
        name="own_second",
    )(table, weight, *parts)


def rim_second_kernel(bricks, subs, chans, owns, route_near, table_near, vectors, rows, weight, down_weight, *refs):
    (even, odd), refs = refs[:2], refs[2:]
    sums, refs = refs[:owns], refs[owns:]
    fars, (out, rim, products, total, slots, seen, route, table, semaphore) = refs[:-9], refs[-9:]
    scalars = Scalars([route_near, table_near], [route, table], semaphore)
    count, reach = table.shape[0], even.shape[0]
    width = weight.shape[1]
    place = Place()
    for j in range(chans):
        near = (even, odd) if j == 0 else (fars[j - 1].at[0:reach], fars[j - 1].at[reach:])
        for c in range(chans):

            @pl.when(lax.rem(place.chan + j, chans) == c)
            def _(near=near, c=c):
                rim_blocks(place, *near, slice(c * width, (c + 1) * width), rim)

    total[...] = sums[0][...]
    for more in sums[1:]:
        total[...] += more[...]

    def end(n, value):
        total[n] = value

    named_sums(table, scalars, rim, weight, products, lambda n: total[n], end)
    for c in range(chans):

        @pl.when(place.chan == c)
        def _(c=c):
            total[...] = (
                total[...] * vectors[2:3][None]
                + vectors[3:4][None]
                + rows[:, :, c * width : (c + 1) * width].astype(F32)
            )

    refined = jnp.maximum(total[...], 0.0).reshape(count, CHILDREN, CELLS, width)
    coarse = None
    for o in range(CHILDREN):
        child = refined[:, o].reshape(count * CELLS, width).astype(BF16)
        product = lax.dot_general(child, down_weight[o], NN, preferred_element_type=F32)
        coarse = product if coarse is None else coarse + product
    slots[...] = jnp.full(slots.shape, ABSENT, F32)
    for owner in range(bricks * subs):
        seen[owner] = 0
    for n in range(count):
        owner = route[0, n]
        slot = seen[owner]
        seen[owner] = slot + 1
        device = owner // subs * (chans * subs) + lax.rem(owner, subs)
        for c in range(chans):
            slots[device + c * subs, pl.ds(pl.multiple_of(slot * CELLS, CELLS), CELLS)] = coarse[
                n * CELLS : (n + 1) * CELLS, c * width : (c + 1) * width
            ]
    out[...] = slots[...].astype(BF16)


def rim_second(route, table, vectors, rows, weight, down_weight, even, odd, sums, fars, bricks, subs, chans, capacity):
    count, reach, width = table.shape[0], even.shape[0], weight.shape[1]
    slots = (bricks * subs * chans, capacity * CELLS, width)
    return pl.pallas_call(
        functools.partial(rim_second_kernel, bricks, subs, chans, len(sums)),
        out_shape=jax.ShapeDtypeStruct(slots, BF16),
        in_specs=[VMEM] * (8 + len(sums) + len(fars)),
        out_specs=VMEM,
        scratch_shapes=rim_scratch(reach, weight)
        + [pltpu.VMEM((count, BLK, width), F32)]
        + [pltpu.VMEM(slots, F32), pltpu.SMEM((bricks * subs,), jnp.int32)]
        + scalar_scratch(route, table),
        compiler_params=LIMIT,
        cost_estimate=cost(2 * reach, weight),
        name="rim_second",
    )(route, table, vectors, rows, weight, down_weight, even, odd, *sums, *fars)


def arrive_kernel(bricks, subs, chans, vectors, parts, out):
    held = []
    for b in range(bricks):
        for s in range(subs):
            coarse = None
            for c in range(chans):
                part = parts[(b * chans + c) * subs + s].astype(F32)
                coarse = part if coarse is None else coarse + part
            held.append(coarse)
    coarse = jnp.concatenate(held, axis=0)
    tiles = jnp.maximum(coarse * vectors[4:5] + vectors[5:6], 0.0)
    tiles = jnp.where(coarse < ABSENT / 2, 0.0, tiles)
    out[0] = tiles.T.astype(BF16)


def arrived_tiles(vectors, parts, bricks, subs, chans):
    slots, width = parts.shape[1:]
    return pl.pallas_call(
        functools.partial(arrive_kernel, bricks, subs, chans),
        out_shape=jax.ShapeDtypeStruct((1, width, bricks * subs * slots), BF16),
        in_specs=[VMEM, VMEM],
        out_specs=VMEM,
        compiler_params=LIMIT,
        name="arrived_tiles",
    )(vectors, parts)


def to_owners(ordered, chans):
    bricks, subs = ordered.shape[:2]
    brick, sub = lax.axis_index("brick"), lax.axis_index("sub")

    def pieces(js):
        column = lax.dynamic_index_in_dim(ordered, lax.rem(sub + js, subs), 1, keepdims=False)
        return jnp.stack(
            [
                lax.dynamic_index_in_dim(column, other(brick, jb, bricks), 0, keepdims=False)
                for jb in range(bricks)
            ]
        )

    by_sub = [pieces(0)]
    for js in range(1, subs):
        by_sub.append(to_ahead(pieces(subs - js), "sub", subs - js))
    stacked = [jnp.stack([piece[jb] for piece in by_sub]) for jb in range(bricks)]
    order = sorted(range(1, bricks), key=lambda jb: (jb % 2 == 0, -jb))
    parts = {(0, 0): stacked[0]}
    for jb in order:
        parts[jb, 0] = across(stacked[jb], jb)
    for jb in [0] + order:
        for j in range(1, chans):
            parts[jb, j] = from_ahead(parts[jb, 0], "chan", j)
    return parts


def body(
    features,
    scan_order,
    kernel_map,
    halo_send,
    down_route,
    conv1_weight,
    conv2_weight,
    down_weight,
    gain_first,
    bias_first,
    gain_second,
    bias_second,
    gain_down,
    bias_down,
):
    bricks, subs, chans = (lax.axis_size(axis) for axis in ("brick", "sub", "chan"))
    owners = bricks * subs
    count, reach = kernel_map.shape[0], halo_send.shape[1]
    channels = features.shape[1]
    ordered = sorted_rows(scan_order, features)
    ordered = ordered.reshape(bricks, subs, features.shape[0] // owners, channels)
    parts = to_owners(ordered, chans)
    chan = lax.axis_index("chan")
    down_route = down_route.reshape(1, count)
    vectors = jnp.stack(
        [gain_first, bias_first, gain_second, bias_second, gain_down, bias_down]
    )
    rows, even, odd = assemble(halo_send, parts, bricks, subs, chans)
    rows = rows.reshape(count, BLK, channels)
    even = owner_pairs(even, 0).reshape(reach, BLK, channels)
    odd = owner_pairs(odd, 1).reshape(reach, BLK, channels)
    outside = jnp.where(kernel_map < count, 2 * reach, kernel_map - count)
    if features.shape[0] // owners == BLK:
        own = None
        for j in range(chans):
            here = (kernel_map < count) & (lax.rem(kernel_map, chans) == lax.rem(chan + j, chans))
            inside = jnp.where(here, lax.div(kernel_map, chans), owners)
            own = pieces_first(inside, conv1_weight, parts, own, j, bricks, subs)
    else:
        own = own_first(kernel_map, rows, conv1_weight)
    hidden, even, odd = rim_first(halo_send, outside, vectors, own, even, odd, conv1_weight)
    others = [from_ahead(hidden, "chan", j) for j in range(1, chans)]
    even, odd = owner_pairs(even, 0), owner_pairs(odd, 1)
    sums = [own_second(kernel_map, conv2_weight, [hidden], 0, chans)]
    rim = pack(even, odd, sums)
    fars = [from_ahead(rim, "chan", j) for j in range(1, chans)]
    if others:
        sums.append(own_second(kernel_map, conv2_weight, others, 1, chans))
    capacity = max(2, 2 * count // owners)
    partial = rim_second(
        down_route,
        outside,
        vectors,
        rows,
        conv2_weight,
        down_weight,
        even,
        odd,
        sums,
        fars,
        bricks,
        subs,
        chans,
        capacity,
    )
    partial = lax.all_to_all(
        partial, ("brick", "chan", "sub"), split_axis=0, concat_axis=0, tiled=True
    )
    return arrived_tiles(vectors, partial, bricks, subs, chans)


def solution(mesh):
    placed = (
        P(("groups", "brick", "chan", "sub"), None),
        P(("groups", "brick", "chan", "sub"), None),
        P(("groups", "brick", "sub"), None),
        P(("groups", "brick", "sub"), None),
        P(("groups", "brick", "sub"), None),
        P(None, "chan", None),
        P(None, "chan", None),
        P(None, "chan", None),
        P("chan"),
        P("chan"),
        P("chan"),
        P("chan"),
        P("chan"),
        P("chan"),
    )
    return jax.shard_map(
        body,
        mesh=mesh,
        in_specs=placed,
        out_specs=P(("groups", "brick", "sub"), "chan", None),
        check_vma=False,
    )
```

```python
import functools

import jax
import jax.numpy as jnp
from jax import lax
from jax.experimental import pallas as pl
from jax.experimental.pallas import tpu as pltpu
from jax.sharding import PartitionSpec as P

BLK = 64
CHILDREN = 8
CELLS = BLK // CHILDREN
ABSENT = -1e30
F32 = jnp.float32
BF16 = jnp.bfloat16
NT = (((1,), (1,)), ((), ()))
NN = (((1,), (0,)), ((), ()))
VMEM = pl.BlockSpec(memory_space=pltpu.VMEM)
LIMIT = pltpu.CompilerParams(vmem_limit_bytes=40 * 2**20)


class Place:
    def __init__(self):
        self.brick, self.sub, self.chan = (lax.axis_index(a) for a in ("brick", "sub", "chan"))
        self.parity = lax.rem(self.brick * lax.axis_size("sub") + self.sub, 2)


class Scalars:
    def __init__(self, given, held, semaphore):
        self.copies = [
            pltpu.make_async_copy(source, target, semaphore.at[i])
            for i, (source, target) in enumerate(zip(given, held))
        ]
        for copy in self.copies:
            copy.start()

    def wait(self):
        for copy in self.copies:
            copy.wait()


def scalar_scratch(*arrays):
    return [pltpu.SMEM(x.shape, jnp.int32) for x in arrays] + [
        pltpu.SemaphoreType.DMA((len(arrays),))
    ]


def owner_pairs(block, parity):
    owners = lax.axis_size("brick") * lax.axis_size("sub")
    pairs = [(o, o + 1) for o in range(parity, owners - 1, 2)]
    if parity == 1 and owners % 2 == 0:
        pairs.append((0, owners - 1))
    return lax.ppermute(block, ("brick", "sub"), pairs + [(b, a) for a, b in pairs])


def named(place, odd):
    owners = lax.axis_size("brick") * lax.axis_size("sub")
    owner = place.brick * lax.axis_size("sub") + place.sub
    inside = (owner > 0) & ((owner < owners - 1) | (place.parity == 0))
    return jnp.where(inside, odd, jnp.zeros_like(odd))


def from_ahead(block, axis, distance):
    n = lax.axis_size(axis)
    return lax.ppermute(block, axis, [((i + distance) % n, i) for i in range(n)])


def other(brick, step, bricks, way=1):
    if bricks & (bricks - 1) == 0:
        return brick ^ step
    return (brick + way * step + bricks) % bricks


def across(block, step):
    bricks = lax.axis_size("brick")
    return lax.ppermute(block, "brick", [(b, other(b, step, bricks)) for b in range(bricks)])


def to_ahead(block, axis, distance):
    n = lax.axis_size(axis)
    return lax.ppermute(block, axis, [(i, (i + distance) % n) for i in range(n)])


def sorted_rows(scan_order, features):
    total = features.shape[0]
    taken = scan_order.reshape(total, 1) == jnp.arange(total, dtype=jnp.int32)[None]
    return jnp.dot(taken.astype(BF16), features, preferred_element_type=F32).astype(BF16)


def assemble_kernel(bricks, subs, chans, keys, halo_near, *refs):
    parts, (rows, even, odd) = dict(zip(keys, refs[:-3])), refs[-3:]
    lists, reach = halo_near[...], halo_near.shape[1]
    place = Place()
    split = BLK // parts[0, 0].shape[1]
    for (jb, j), part in parts.items():
        source = other(place.brick, jb, bricks, -1)
        chan = lax.rem(place.chan + j, chans)
        for js in range(subs):
            sub = lax.rem(place.sub + js, subs)
            rows[(source * subs + sub) * chans + chan] = part[js]
    for j in range(reach):
        up, down = lists[0, j], lists[1, j]
        first = jnp.where(place.parity == 0, up, down)
        second = jnp.where(place.parity == 0, down, up)
        even[pl.ds(j * split, split)] = rows[pl.ds(first * split, split)]
        odd[pl.ds(j * split, split)] = rows[pl.ds(second * split, split)]


def assemble(halo, parts, bricks, subs, chans):
    per, channels = parts[0, 0].shape[1:]
    pieces = bricks * subs * chans
    split = BLK // per
    sent = halo.shape[1] * split
    return pl.pallas_call(
        functools.partial(assemble_kernel, bricks, subs, chans, tuple(parts)),
        out_shape=[
            jax.ShapeDtypeStruct((count, per, channels), BF16) for count in (pieces, sent, sent)
        ],
        in_specs=[VMEM] * (1 + len(parts)),
        out_specs=[VMEM] * 3,
        compiler_params=LIMIT,
        name="assemble",
    )(halo, *parts.values())


def block_sums(table, blocks, weight, total):
    count = table.shape[0]
    group = min(count, 16)
    lanes = blocks.shape[2]
    offsets = weight.shape[2] // lanes

    def one_group(g, carry):
        first = g * group
        running = None
        for w in range(weight.shape[0]):
            inside = range(w * offsets, min((w + 1) * offsets, table.shape[1]))
            picked = jnp.concatenate(
                [
                    jnp.concatenate(
                        [blocks[jnp.minimum(table[first + n, k], count)] for k in inside], axis=1
                    )
                    for n in range(group)
                ],
                axis=0,
            )
            product = lax.dot_general(
                picked, weight[w, :, : len(inside) * lanes], NT, preferred_element_type=F32
            )
            running = product if running is None else running + product
        total[pl.ds(first, group)] = running.reshape(group, BLK, weight.shape[1])
        return carry

    if count == group:
        one_group(0, 0)
    else:
        lax.fori_loop(0, count // group, one_group, 0)


def rim_blocks(place, even, odd, lanes, rim):
    reach = even.shape[0]
    rim[pl.ds(reach * (1 - place.parity), reach), :, lanes] = even[...]
    rim[pl.ds(reach * place.parity, reach), :, lanes] = named(place, odd[...])


def named_sums(table, scalars, given, weight, products, begin, end):
    blocks, offsets = given.shape[0], table.shape[1]
    width, channels = weight.shape[1:]
    together = max(1, channels // width)
    rows = given[...].reshape(blocks * BLK, channels)
    for k in range(0, offsets, together):
        size = min(together, offsets - k)
        product = lax.dot_general(
            rows,
            weight[k : k + size].reshape(size * width, channels),
            NT,
            preferred_element_type=F32,
        )
        for i in range(size):
            products[k + i, 0:blocks] = product[:, i * width : (i + 1) * width].reshape(
                blocks, BLK, width
            )
    products[:, blocks : blocks + 1] = jnp.zeros((offsets, 1, BLK, width), F32)
    scalars.wait()

    def one_block(n, carry):
        running = begin(n)
        for k in range(offsets):
            running = running + products[k, table[n, k]]
        end(n, running)
        return carry

    lax.fori_loop(0, table.shape[0], one_block, 0, unroll=min(table.shape[0], 16))


def cost(blocks, weight):
    offsets, width, channels = weight.shape
    return pl.CostEstimate(
        flops=4 * blocks * BLK * offsets * width * channels, bytes_accessed=0, transcendentals=0
    )


def own_first_kernel(table_near, rows, weight, total, blocks, table, semaphore):
    scalars = Scalars([table_near], [table], semaphore)
    count = rows.shape[0]
    blocks[0:count] = rows[...]
    blocks[count] = jnp.zeros(blocks.shape[1:], BF16)
    scalars.wait()
    block_sums(table, blocks, weight, total)


def own_first(table, rows, weight):
    count, channels = rows.shape[0], rows.shape[2]
    return pl.pallas_call(
        own_first_kernel,
        out_shape=jax.ShapeDtypeStruct((count, BLK, weight.shape[1]), F32),
        in_specs=[VMEM] * 3,
        out_specs=VMEM,
        scratch_shapes=[pltpu.VMEM((count + 1, BLK, channels), BF16)] + scalar_scratch(table),
        compiler_params=LIMIT,
        cost_estimate=cost(count, weight),
        name="own_first",
    )(table, rows, weight)


def pieces_first_kernel(bricks, subs, behind, started, table_near, weight, *refs):
    parts, (total, held, products, table, semaphore) = refs[:-5], refs[-5:]
    scalars = Scalars([table_near], [table], semaphore)
    if started:
        parts, before = parts[:-1], parts[-1]
    place = Place()
    for jb, part in zip(behind, parts):
        source = other(place.brick, jb, bricks, -1)
        for js in range(subs):
            held[source * subs + lax.rem(place.sub + js, subs)] = part[js]

    def begin(n):
        return before[n] if started else jnp.zeros(total.shape[1:], F32)

    def end(n, value):
        total[n] = value

    named_sums(table, scalars, held, weight, products, begin, end)


def pieces_first(table, weight, parts, before, j, bricks, subs):
    offsets, width, channels = weight.shape
    sums = jax.ShapeDtypeStruct((table.shape[0], BLK, width), F32)
    held = bricks * subs
    behind = tuple(jb for jb, far in parts if far == j)
    given = [parts[jb, j] for jb in behind] + ([] if before is None else [before])
    return pl.pallas_call(
        functools.partial(pieces_first_kernel, bricks, subs, behind, before is not None),
        out_shape=sums,
        in_specs=[VMEM] * (2 + len(given)),
        out_specs=VMEM,
        scratch_shapes=[
            pltpu.VMEM((held, BLK, channels), BF16),
            pltpu.VMEM((offsets, held + 1, BLK, width), F32),
        ]
        + scalar_scratch(table),
        compiler_params=LIMIT,
        cost_estimate=cost(held, weight),
        name="pieces_first",
    )(table, weight, *given)


def rim_first_kernel(odd, even, halo_near, table_near, vectors, own, weight, *refs):
    hidden, even_out, odd_out, rim, products, halo, table, semaphore = refs
    scalars = Scalars([halo_near, table_near], [halo, table], semaphore)
    reach = even.shape[0]
    place = Place()
    rim_blocks(place, even, odd, slice(None), rim)
    gain, bias = vectors[0:1], vectors[1:2]

    def end(n, value):
        hidden[n] = jnp.maximum(value * gain + bias, 0.0).astype(BF16)

    named_sums(table, scalars, rim, weight, products, lambda n: own[n], end)
    for j in range(reach):
        even_out[j] = hidden[halo[place.parity, j]]
        odd_out[j] = hidden[halo[1 - place.parity, j]]


def rim_scratch(reach, weight):
    offsets, width, channels = weight.shape
    return [
        pltpu.VMEM((2 * reach, BLK, channels), BF16),
        pltpu.VMEM((offsets, 2 * reach + 1, BLK, width), F32),
    ]


def rim_first(halo, table, vectors, own, even, odd, weight):
    count, reach, width = table.shape[0], even.shape[0], weight.shape[1]
    return pl.pallas_call(
        rim_first_kernel,
        out_shape=[
            jax.ShapeDtypeStruct((n, BLK, width), BF16) for n in (count, reach, reach)
        ],
        in_specs=[VMEM] * 7,
        out_specs=[VMEM] * 3,
        scratch_shapes=rim_scratch(reach, weight) + scalar_scratch(halo, table),
        compiler_params=LIMIT,
        cost_estimate=cost(2 * reach, weight),
        name="rim_first",
    )(odd, even, halo, table, vectors, own, weight)


def pack_kernel(even, odd, *refs):
    out = refs[-1]
    out[0 : even.shape[0]] = even[...]
    out[even.shape[0] :] = odd[...]


def pack(even, odd, after):
    return pl.pallas_call(
        pack_kernel,
        out_shape=jax.ShapeDtypeStruct((2 * even.shape[0],) + even.shape[1:], BF16),
        in_specs=[VMEM, VMEM] + [pl.BlockSpec(memory_space=pl.ANY)] * len(after),
        out_specs=VMEM,
        compiler_params=LIMIT,
        name="pack",
    )(even, odd, *after)


def own_second_kernel(nearest, chans, table_near, weight, *refs):
    parts, (total, blocks, beside, table, semaphore) = refs[:-5], refs[-5:]
    scalars = Scalars([table_near], [table], semaphore)
    count, width = parts[0].shape[0], parts[0].shape[2]
    place = Place()
    lanes = blocks.shape[2]
    offsets = beside.shape[2] // lanes
    for i, part in enumerate(parts):
        blocks[0:count, :, i * width : (i + 1) * width] = part[...]
        for c in range(chans):

            @pl.when(lax.rem(place.chan + nearest + i, chans) == c)
            def _(i=i, c=c):
                for k in range(weight.shape[0]):
                    at = k % offsets * lanes + i * width
                    beside[k // offsets, :, at : at + width] = weight[
                        k, :, c * width : (c + 1) * width
                    ]

    blocks[count] = jnp.zeros(blocks.shape[1:], BF16)
    scalars.wait()
    block_sums(table, blocks, beside, total)


def own_second(table, weight, parts, nearest, chans):
    count, width = parts[0].shape[0], parts[0].shape[2]
    lanes = width * len(parts)
    offsets = max(1, weight.shape[2] // lanes)
    groups = -(-weight.shape[0] // offsets)
    return pl.pallas_call(
        functools.partial(own_second_kernel, nearest, chans),
        out_shape=jax.ShapeDtypeStruct((count, BLK, width), F32),
        in_specs=[VMEM] * (2 + len(parts)),
        out_specs=VMEM,
        scratch_shapes=[
            pltpu.VMEM((count + 1, BLK, lanes), BF16),
            pltpu.VMEM((groups, width, lanes * offsets), BF16),
        ]
        + scalar_scratch(table),
        compiler_params=LIMIT,
        cost_estimate=cost(count // 2, weight),
        name="own_second",
    )(table, weight, *parts)


def rim_second_kernel(bricks, subs, chans, owns, route_near, table_near, vectors, rows, weight, down_weight, *refs):
    (even, odd), refs = refs[:2], refs[2:]
    sums, refs = refs[:owns], refs[owns:]
    fars, (out, rim, products, total, slots, seen, route, table, semaphore) = refs[:-9], refs[-9:]
    scalars = Scalars([route_near, table_near], [route, table], semaphore)
    count, reach = table.shape[0], even.shape[0]
    width = weight.shape[1]
    place = Place()
    for j in range(chans):
        near = (even, odd) if j == 0 else (fars[j - 1].at[0:reach], fars[j - 1].at[reach:])
        for c in range(chans):

            @pl.when(lax.rem(place.chan + j, chans) == c)
            def _(near=near, c=c):
                rim_blocks(place, *near, slice(c * width, (c + 1) * width), rim)

    total[...] = sums[0][...]
    for more in sums[1:]:
        total[...] += more[...]

    def end(n, value):
        total[n] = value

    named_sums(table, scalars, rim, weight, products, lambda n: total[n], end)
    for c in range(chans):

        @pl.when(place.chan == c)
        def _(c=c):
            total[...] = (
                total[...] * vectors[2:3][None]
                + vectors[3:4][None]
                + rows[:, :, c * width : (c + 1) * width].astype(F32)
            )

    refined = jnp.maximum(total[...], 0.0).reshape(count, CHILDREN, CELLS, width)
    beside = jnp.concatenate(
        [refined[:, o].reshape(count * CELLS, width) for o in range(CHILDREN)], axis=1
    ).astype(BF16)
    down = down_weight[...].reshape(CHILDREN * width, down_weight.shape[2])
    coarse = lax.dot_general(beside, down, NN, preferred_element_type=F32)
    slots[...] = jnp.full(slots.shape, ABSENT, F32)
    for owner in range(bricks * subs):
        seen[owner] = 0
    for n in range(count):
        owner = route[0, n]
        slot = seen[owner]
        seen[owner] = slot + 1
        device = owner // subs * (chans * subs) + lax.rem(owner, subs)
        for c in range(chans):
            slots[device + c * subs, pl.ds(pl.multiple_of(slot * CELLS, CELLS), CELLS)] = coarse[
                n * CELLS : (n + 1) * CELLS, c * width : (c + 1) * width
            ]
    out[...] = slots[...].astype(BF16)


def rim_second(route, table, vectors, rows, weight, down_weight, even, odd, sums, fars, bricks, subs, chans, capacity):
    count, reach, width = table.shape[0], even.shape[0], weight.shape[1]
    slots = (bricks * subs * chans, capacity * CELLS, width)
    return pl.pallas_call(
        functools.partial(rim_second_kernel, bricks, subs, chans, len(sums)),
        out_shape=jax.ShapeDtypeStruct(slots, BF16),
        in_specs=[VMEM] * (8 + len(sums) + len(fars)),
        out_specs=VMEM,
        scratch_shapes=rim_scratch(reach, weight)
        + [pltpu.VMEM((count, BLK, width), F32)]
        + [pltpu.VMEM(slots, F32), pltpu.SMEM((bricks * subs,), jnp.int32)]
        + scalar_scratch(route, table),
        compiler_params=LIMIT,
        cost_estimate=cost(2 * reach, weight),
        name="rim_second",
    )(route, table, vectors, rows, weight, down_weight, even, odd, *sums, *fars)


def arrive_kernel(bricks, subs, chans, vectors, parts, out):
    held = []
    for b in range(bricks):
        for s in range(subs):
            coarse = None
            for c in range(chans):
                part = parts[(b * chans + c) * subs + s].astype(F32)
                coarse = part if coarse is None else coarse + part
            held.append(coarse)
    coarse = jnp.concatenate(held, axis=0)
    tiles = jnp.maximum(coarse * vectors[4:5] + vectors[5:6], 0.0)
    tiles = jnp.where(coarse < ABSENT / 2, 0.0, tiles)
    out[0] = tiles.T.astype(BF16)


def arrived_tiles(vectors, parts, bricks, subs, chans):
    slots, width = parts.shape[1:]
    return pl.pallas_call(
        functools.partial(arrive_kernel, bricks, subs, chans),
        out_shape=jax.ShapeDtypeStruct((1, width, bricks * subs * slots), BF16),
        in_specs=[VMEM, VMEM],
        out_specs=VMEM,
        compiler_params=LIMIT,
        name="arrived_tiles",
    )(vectors, parts)


def to_owners(ordered, chans):
    bricks, subs = ordered.shape[:2]
    brick, sub = lax.axis_index("brick"), lax.axis_index("sub")

    def pieces(js):
        column = lax.dynamic_index_in_dim(ordered, lax.rem(sub + js, subs), 1, keepdims=False)
        return jnp.stack(
            [
                lax.dynamic_index_in_dim(column, other(brick, jb, bricks), 0, keepdims=False)
                for jb in range(bricks)
            ]
        )

    by_sub = [pieces(0)]
    for js in range(1, subs):
        by_sub.append(to_ahead(pieces(subs - js), "sub", subs - js))
    stacked = [jnp.stack([piece[jb] for piece in by_sub]) for jb in range(bricks)]
    order = sorted(range(1, bricks), key=lambda jb: (jb % 2 == 0, -jb))
    parts = {(0, 0): stacked[0]}
    for jb in order:
        parts[jb, 0] = across(stacked[jb], jb)
    for jb in [0] + order:
        for j in range(1, chans):
            parts[jb, j] = from_ahead(parts[jb, 0], "chan", j)
    return parts


def body(
    features,
    scan_order,
    kernel_map,
    halo_send,
    down_route,
    conv1_weight,
    conv2_weight,
    down_weight,
    gain_first,
    bias_first,
    gain_second,
    bias_second,
    gain_down,
    bias_down,
):
    bricks, subs, chans = (lax.axis_size(axis) for axis in ("brick", "sub", "chan"))
    owners = bricks * subs
    count, reach = kernel_map.shape[0], halo_send.shape[1]
    channels = features.shape[1]
    ordered = sorted_rows(scan_order, features)
    ordered = ordered.reshape(bricks, subs, features.shape[0] // owners, channels)
    parts = to_owners(ordered, chans)
    chan = lax.axis_index("chan")
    down_route = down_route.reshape(1, count)
    vectors = jnp.stack(
        [gain_first, bias_first, gain_second, bias_second, gain_down, bias_down]
    )
    rows, even, odd = assemble(halo_send, parts, bricks, subs, chans)
    rows = rows.reshape(count, BLK, channels)
    even = owner_pairs(even, 0).reshape(reach, BLK, channels)
    odd = owner_pairs(odd, 1).reshape(reach, BLK, channels)
    outside = jnp.where(kernel_map < count, 2 * reach, kernel_map - count)
    if features.shape[0] // owners == BLK:
        own = None
        for j in range(chans):
            here = (kernel_map < count) & (lax.rem(kernel_map, chans) == lax.rem(chan + j, chans))
            inside = jnp.where(here, lax.div(kernel_map, chans), owners)
            own = pieces_first(inside, conv1_weight, parts, own, j, bricks, subs)
    else:
        own = own_first(kernel_map, rows, conv1_weight)
    hidden, even, odd = rim_first(halo_send, outside, vectors, own, even, odd, conv1_weight)
    others = [from_ahead(hidden, "chan", j) for j in range(1, chans)]
    even, odd = owner_pairs(even, 0), owner_pairs(odd, 1)
    sums = [own_second(kernel_map, conv2_weight, [hidden], 0, chans)]
    rim = pack(even, odd, sums)
    fars = [from_ahead(rim, "chan", j) for j in range(1, chans)]
    if others:
        sums.append(own_second(kernel_map, conv2_weight, others, 1, chans))
    capacity = max(2, 2 * count // owners)
    partial = rim_second(
        down_route,
        outside,
        vectors,
        rows,
        conv2_weight,
        down_weight,
        even,
        odd,
        sums,
        fars,
        bricks,
        subs,
        chans,
        capacity,
    )
    partial = lax.all_to_all(
        partial, ("brick", "chan", "sub"), split_axis=0, concat_axis=0, tiled=True
    )
    return arrived_tiles(vectors, partial, bricks, subs, chans)


def solution(mesh):
    placed = (
        P(("groups", "brick", "chan", "sub"), None),
        P(("groups", "brick", "chan", "sub"), None),
        P(("groups", "brick", "sub"), None),
        P(("groups", "brick", "sub"), None),
        P(("groups", "brick", "sub"), None),
        P(None, "chan", None),
        P(None, "chan", None),
        P(None, "chan", None),
        P("chan"),
        P("chan"),
        P("chan"),
        P("chan"),
        P("chan"),
        P("chan"),
    )
    return jax.shard_map(
        body,
        mesh=mesh,
        in_specs=placed,
        out_specs=P(("groups", "brick", "sub"), "chan", None),
        check_vma=False,
    )
```
